256 devices in a mesh: src: 32 (over z, x), tgt: 8 (over y, core).
Axes of the slice: x: 4, y: 4, z: 8, core: 2. Of those that a mesh axis runs over, the one named last changes fastest.
Arguments:
- sources: bfloat16 [65536, 768], P('src'), may hold values from -24 to 24
- targets: bfloat16 [32768, 768], P('tgt'), may hold values from -24 to 24
- block_lists: int32 [256, 8, 4], P('src', 'tgt'), may hold values from 0 to 15, as said below
- live_counts: int32 [256, 8], P('src', 'tgt'), may hold values from 1 to 4, as said below
Outputs:
- mapped_rows: float32 [65536, 768], P(('src', 'tgt'))
- row_potential: float32 [65536], P('src')
- col_potential: float32 [32768], P('tgt')
The draws below stay inside these ranges and needn't reach their ends.
Inputs may be any that keep to these rules, and one draw needn't show every extreme that they name: `block_lists`: entries of a list at one (b, t) are distinct block numbers within shard t; every target block of every shard is the first entry of the list of some source block. `live_counts`: some list is full in every draw.
All inputs are finite; a program needn't handle non-finite values.
Results may differ from the reference program's by a relative error of at most 0.007.
Values sent between devices are 32-bit elements; how exact they have to be, the bound alone decides.
No kernel may reach another device: no remote copies, remote signals or barrier semaphores. Data moves between devices by JAX's collectives and lax.ppermute only.
A program may use at most 128 MiB of HBM per device.

```python
import math
import jax
import jax.numpy as jnp
from jax import lax

D = 768
BLK = 256
CAP = 4
ITERS = 3
TB = 16
NSB = 256
NTB = 128
NS = 65536
NT = 32768
N_TGT = 8


def draw_sources(key, part):
    key = jax.random.fold_in(key, 21)
    first_key = jax.random.fold_in(key, 0)
    values = jax.random.truncated_normal(first_key, -4.0, 4.0, (NS, D), jnp.float32)
    return values.astype(jnp.bfloat16)


def draw_targets(key, part):
    key = jax.random.fold_in(key, 37)
    first_key = jax.random.fold_in(key, 0)
    values = jax.random.truncated_normal(first_key, -4.0, 4.0, (NT, D), jnp.float32)
    return values.astype(jnp.bfloat16)


def draw_block_lists(key, part):
    key = jax.random.fold_in(key, 11)
    first_key, second_key = jax.random.split(key)
    shuffles = jax.vmap(lambda one_key: jax.random.permutation(one_key, TB))(jax.random.split(first_key, N_TGT))
    offset = jax.random.randint(second_key, (NSB, N_TGT), 0, TB - CAP + 1)
    block = jnp.arange(NSB, dtype=jnp.int32)[:, None, None]
    slot = jnp.arange(CAP, dtype=jnp.int32)[None, None, :]
    position = jnp.where(slot == 0, block % TB, (block + offset[:, :, None] + slot) % TB)
    shard = jnp.broadcast_to(jnp.arange(N_TGT, dtype=jnp.int32)[None, :, None], position.shape)
    return shuffles[shard, position].astype(jnp.int32)


def draw_live_counts(key, part):
    key = jax.random.fold_in(key, 53)
    first_key, second_key, third_key = jax.random.split(key, 3)
    lower = jnp.minimum(jax.random.randint(first_key, (NSB, N_TGT), 1, CAP + 1), jax.random.randint(second_key, (NSB, N_TGT), 1, CAP + 1))
    chosen = jax.random.randint(third_key, (), 0, NSB * N_TGT)
    flat = jnp.arange(NSB * N_TGT, dtype=jnp.int32).reshape(NSB, N_TGT)
    return jnp.where(flat == chosen, CAP, lower).astype(jnp.int32)


def setup_inputs(seed: int = 0) -> dict:
    keys = jax.random.split(jax.random.key(seed), 5)
    sources = draw_sources(jax.random.fold_in(keys[4], 71), 0)
    targets = draw_targets(jax.random.fold_in(keys[4], 71), 0)
    block_lists = draw_block_lists(jax.random.fold_in(keys[4], 71), 0)
    live_counts = draw_live_counts(jax.random.fold_in(keys[4], 71), 0)
    return {"sources": sources, "targets": targets, "block_lists": block_lists, "live_counts": live_counts}


EPSILON = 0.1
NEGATIVE = -1e30


def reference(sources, targets, block_lists, live_counts):
    src_tiles = sources.reshape(NSB, BLK, D)
    tgt_tiles = targets.reshape(NTB, BLK, D)
    target_ids = (jnp.arange(N_TGT, dtype=jnp.int32)[None, :, None] * TB + block_lists).reshape(NSB, N_TGT * CAP).astype(jnp.int32)
    live_slot = (jnp.arange(CAP, dtype=jnp.int32)[None, None, :] < live_counts[:, :, None]).reshape(NSB, N_TGT * CAP)
    src_square = jnp.sum(jnp.square(sources.astype(jnp.float32)), -1).reshape(NSB, BLK)
    tgt_square = jnp.sum(jnp.square(targets.astype(jnp.float32)), -1).reshape(NTB, BLK)

    def tile_costs(block):
        ids = target_ids[block]
        cross_term = jnp.einsum("rd,lcd->lrc", src_tiles[block].astype(jnp.float32), tgt_tiles[ids].astype(jnp.float32))
        return (src_square[block][None, :, None] + tgt_square[ids][:, None, :] - 2.0 * cross_term) / D

    tile_cost = lax.map(tile_costs, jnp.arange(NSB, dtype=jnp.int32))
    live_mask = live_slot[:, :, None, None]
    flat_ids = target_ids.reshape(-1)

    def row_logsum(col_potential):
        scores = jnp.where(live_mask, (col_potential.reshape(NTB, BLK)[target_ids][:, :, None, :] - tile_cost) / EPSILON, NEGATIVE)
        peak = jnp.max(scores, axis=(1, 3))
        summed = jnp.sum(jnp.exp(scores - peak[:, None, :, None]), axis=(1, 3))
        return scores, peak + jnp.log(summed)

    col_potential = jnp.zeros((NT,), jnp.float32)
    row_potential = jnp.zeros((NSB, BLK), jnp.float32)
    for sweep in range(ITERS):
        scores, row_lse = row_logsum(col_potential)
        row_potential = -EPSILON * math.log(NS) - EPSILON * row_lse
        scores = jnp.where(live_mask, (row_potential[:, None, :, None] - tile_cost) / EPSILON, NEGATIVE)
        tile_max = jnp.where(live_slot[:, :, None], jnp.max(scores, axis=2), NEGATIVE)
        col_peak = jnp.full((NTB, BLK), NEGATIVE, jnp.float32).at[flat_ids].max(tile_max.reshape(-1, BLK))
        tile_sum = jnp.sum(jnp.exp(scores - col_peak[target_ids][:, :, None, :]), axis=2)
        tile_sum = jnp.where(live_slot[:, :, None], tile_sum, 0.0)
        col_summed = jnp.zeros((NTB, BLK), jnp.float32).at[flat_ids].add(tile_sum.reshape(-1, BLK))
        col_potential = (-EPSILON * math.log(NT) - EPSILON * (col_peak + jnp.log(col_summed))).reshape(NT)
    scores, final_lse = row_logsum(col_potential)
    weights = jnp.where(live_mask, jnp.exp(scores - final_lse[:, None, :, None]), 0.0).astype(jnp.bfloat16)

    def project(block):
        return jnp.einsum("lrc,lcd->rd", weights[block].astype(jnp.float32), tgt_tiles[target_ids[block]].astype(jnp.float32))

    numerator = lax.map(project, jnp.arange(NSB, dtype=jnp.int32))
    mapped_rows = numerator.reshape(NS, D)
    return mapped_rows, row_potential.reshape(NS), col_potential
```

```python
import functools
import math

import jax
import jax.numpy as jnp
from jax import lax
from jax.experimental import pallas as pl
from jax.experimental.pallas import tpu as pltpu
from jax.sharding import PartitionSpec as P

BLK = 256
ITERS = 3
EPSILON = 0.1
NEGATIVE = -1e30
LOG2E = math.log2(math.e)
LN2 = math.log(2.0)
LANES = 128

VMEM = pl.BlockSpec(memory_space=pltpu.VMEM)
SMEM = pl.BlockSpec(memory_space=pltpu.SMEM)
ANY = pl.BlockSpec(memory_space=pl.ANY)
PARAMS = pltpu.CompilerParams(vmem_limit_bytes=40 * 1024 * 1024)


def eye():
    shape = (LANES, LANES)
    return lax.broadcasted_iota(jnp.int32, shape, 0) == lax.broadcasted_iota(jnp.int32, shape, 1)


def to_lanes(column):
    mask = eye()
    halves = [
        jnp.sum(jnp.where(mask, column[h * LANES : (h + 1) * LANES], 0.0), axis=0, keepdims=True)
        for h in range(BLK // LANES)
    ]
    return jnp.concatenate(halves, axis=1)


def to_sublanes(row):
    mask = eye()
    halves = [
        jnp.sum(jnp.where(mask, row[:, h * LANES : (h + 1) * LANES], 0.0), axis=1, keepdims=True)
        for h in range(BLK // LANES)
    ]
    return jnp.concatenate(halves, axis=0)


def fold_rows(tile, op):
    out = tile[0:8]
    for r in range(8, BLK, 8):
        out = op(out, tile[r : r + 8])
    return out


def merge_lse(ref):
    values = ref[...]
    peak = jnp.max(values, axis=0)
    return peak + jnp.log2(jnp.sum(jnp.exp2(values - peak[None]), axis=0))


def cost_kernel(lists, counts, src_hbm, tgt_hbm, tgt, z_ref, rows, src, bias, sems, *, features):
    tgt_blocks, src_blocks = tgt.shape[0], src.shape[0]
    src_copies = [
        pltpu.make_async_copy(src_hbm.at[b], src.at[b], sems.at[tgt_blocks + b])
        for b in range(src_blocks)
    ]
    tgt_copies = [
        pltpu.make_async_copy(tgt_hbm.at[t], tgt.at[t], sems.at[t]) for t in range(tgt_blocks)
    ]
    for copy in tgt_copies:
        copy.start()
    for copy in src_copies:
        copy.start()
    scale = LOG2E / (features * EPSILON)
    mask = eye()
    for t in range(tgt_blocks):
        tgt_copies[t].wait()
        for h in range(BLK // LANES):
            part = tgt[t, h * LANES : (h + 1) * LANES, :]
            gram = lax.dot_general(
                part, part, (((1,), (1,)), ((), ())), preferred_element_type=jnp.float32
            )
            square = jnp.sum(jnp.where(mask, gram, 0.0), axis=0, keepdims=True)
            bias[t : t + 1, h * LANES : (h + 1) * LANES] = -scale * square
    for b in range(src_blocks):
        src_copies[b].wait()

        def score(k, peak, b=b):
            t = lists[b, k]
            cross = lax.dot_general(
                src[b], tgt[t], (((1,), (1,)), ((), ())), preferred_element_type=jnp.float32
            )
            z = (2.0 * scale) * cross + bias[pl.ds(t, 1), :]
            z_ref[b, k] = z
            return jnp.maximum(peak, jnp.maximum(z[:, :LANES], z[:, LANES:]))

        count = counts[b]
        peak = lax.fori_loop(0, count, score, jnp.full((BLK, LANES), NEGATIVE, jnp.float32))
        peak = jnp.max(peak, axis=1, keepdims=True)

        def total(k, acc, b=b, peak=peak):
            e = jnp.exp2(z_ref[b, k] - peak)
            return acc + e[:, :LANES] + e[:, LANES:]

        acc = lax.fori_loop(0, count, total, jnp.zeros((BLK, LANES), jnp.float32))
        lse = peak + jnp.log2(jnp.sum(acc, axis=1, keepdims=True))
        rows[b : b + 1, :] = to_lanes(lse)


def first_col_kernel(lists, counts, z_ref, row_parts, w_ref, row_lse, cols, peaks, sums):
    src_blocks, tgt_blocks = z_ref.shape[0], cols.shape[0]
    row_lse[...] = merge_lse(row_parts)
    peaks[...] = jnp.full(peaks.shape, NEGATIVE, jnp.float32)
    sums[...] = jnp.zeros(sums.shape, jnp.float32)
    for b in range(src_blocks):
        shift = to_sublanes(row_lse[b : b + 1, :])

        def shifted(k, carry, b=b, shift=shift):
            t = lists[b, k]
            w = z_ref[b, k] - shift
            w_ref[b, k] = w
            peaks[t] = jnp.maximum(peaks[t], fold_rows(w, jnp.maximum))
            return carry

        lax.fori_loop(0, counts[b], shifted, 0)
    for t in range(tgt_blocks):
        peaks[t] = jnp.broadcast_to(jnp.max(peaks[t], axis=0, keepdims=True), (8, BLK))
    for b in range(src_blocks):

        def summed(k, carry, b=b):
            t = lists[b, k]
            e = jnp.exp2(w_ref[b, k] - peaks[t, 0:1, :])
            sums[t] += fold_rows(e, jnp.add)
            return carry

        lax.fori_loop(0, counts[b], summed, 0)
    for t in range(tgt_blocks):
        total = jnp.sum(sums[t], axis=0, keepdims=True)
        lse = peaks[t, 0:1, :] + jnp.log2(total)
        cols[t : t + 1, :] = jnp.where(total > 0.0, lse, NEGATIVE)


def row_totals(lists, counts, tile, rows, src_blocks):
    for b in range(src_blocks):

        def total(k, acc, b=b):
            q = tile(b, k, lists[b, k])
            return acc + q[:, :LANES] + q[:, LANES:]

        acc = lax.fori_loop(0, counts[b], total, jnp.zeros((BLK, LANES), jnp.float32))
        rows[b : b + 1, :] = to_lanes(jnp.sum(acc, axis=1, keepdims=True))


def first_row_kernel(lists, counts, w_ref, col_parts, q_ref, col_lse, rows):
    col_lse[...] = merge_lse(col_parts)

    def tile(b, k, t):
        q = jnp.exp2(w_ref[b, k] - col_lse[pl.ds(t, 1), :])
        q_ref[b, k] = q
        return q

    row_totals(lists, counts, tile, rows, w_ref.shape[0])


def col_kernel(lists, counts, q_ref, row_parts, row_scale, cols, sums, *, share):
    src_blocks, tgt_blocks = q_ref.shape[0], cols.shape[0]
    row_scale[...] = share / jnp.sum(row_parts[...], axis=0)
    sums[...] = jnp.zeros(sums.shape, jnp.float32)
    for b in range(src_blocks):
        scale = to_sublanes(row_scale[b : b + 1, :])

        def summed(k, carry, b=b, scale=scale):
            t = lists[b, k]
            sums[t] += fold_rows(q_ref[b, k] * scale, jnp.add)
            return carry

        lax.fori_loop(0, counts[b], summed, 0)
    for t in range(tgt_blocks):
        cols[t : t + 1, :] = jnp.sum(sums[t], axis=0, keepdims=True)


def row_kernel(lists, counts, q_ref, col_parts, col_scale, rows):
    col_scale[...] = 1.0 / jnp.sum(col_parts[...], axis=0)

    def tile(b, k, t):
        return q_ref[b, k] * col_scale[pl.ds(t, 1), :]

    row_totals(lists, counts, tile, rows, q_ref.shape[0])


def project_kernel(lists, counts, q_ref, col_parts, tgt, col_scale, out, rows):
    col_scale[...] = 1.0 / jnp.sum(col_parts[...], axis=0)
    for b in range(q_ref.shape[0]):

        def project(k, acc, b=b):
            t = lists[b, k]
            weights = q_ref[b, k] * col_scale[pl.ds(t, 1), :]
            part = jnp.dot(
                weights.astype(jnp.bfloat16), tgt[t], preferred_element_type=jnp.float32
            )

            @pl.when(k == 0)
            def _():
                out[b] = part

            @pl.when(k > 0)
            def _():
                out[b] += part

            return acc + weights[:, :LANES] + weights[:, LANES:]

        acc = lax.fori_loop(0, counts[b], project, jnp.zeros((BLK, LANES), jnp.float32))
        rows[b : b + 1, :] = to_lanes(jnp.sum(acc, axis=1, keepdims=True))


def in_vmem(x):
    return pltpu.with_memory_space_constraint(x, pltpu.VMEM)


def f32(*shape):
    return jax.ShapeDtypeStruct(shape, jnp.float32)


def gather(x, axis):
    n = lax.axis_size(axis)
    return lax.all_to_all(jnp.broadcast_to(x[None], (n, *x.shape)), axis, 0, 0)


def local(sources, targets, block_lists, live_counts):
    src_rows, features = sources.shape
    src_blocks = src_rows // BLK
    tgt_blocks = targets.shape[0] // BLK
    slots = block_lists.shape[2]
    lists = block_lists[:, 0, :]
    counts = live_counts[:, 0]
    total_src = src_rows * lax.axis_size("src")
    total_tgt = targets.shape[0] * lax.axis_size("tgt")
    src_blocked = sources.reshape(src_blocks, BLK, features)
    tgt_blocked = targets.reshape(tgt_blocks, BLK, features)
    tiles = pltpu.VMEM((src_blocks, slots, BLK, BLK), jnp.float32)
    row_shape, col_shape = f32(src_blocks, BLK), f32(tgt_blocks, BLK)
    col_scratch = pltpu.VMEM((tgt_blocks, 8, BLK), jnp.float32)

    tgt_vmem, z, rows = pl.pallas_call(
        functools.partial(cost_kernel, features=features),
        in_specs=[SMEM, SMEM, ANY, ANY],
        out_specs=[VMEM, VMEM, VMEM],
        out_shape=[pltpu.VMEM(tgt_blocked.shape, jnp.bfloat16), tiles, row_shape],
        scratch_shapes=[
            pltpu.VMEM(src_blocked.shape, jnp.bfloat16),
            pltpu.VMEM((tgt_blocks, BLK), jnp.float32),
            pltpu.SemaphoreType.DMA((tgt_blocks + src_blocks,)),
        ],
        compiler_params=PARAMS,
    )(lists, counts, src_blocked, tgt_blocked)

    w, row_lse, cols = pl.pallas_call(
        first_col_kernel,
        in_specs=[SMEM, SMEM, VMEM, VMEM],
        out_specs=[VMEM, VMEM, VMEM],
        out_shape=[tiles, row_shape, col_shape],
        scratch_shapes=[col_scratch, col_scratch],
        input_output_aliases={2: 0},
        compiler_params=PARAMS,
    )(lists, counts, in_vmem(z), gather(rows, "tgt"))

    q, col_lse, rows = pl.pallas_call(
        first_row_kernel,
        in_specs=[SMEM, SMEM, VMEM, VMEM],
        out_specs=[VMEM, VMEM, VMEM],
        out_shape=[tiles, col_shape, row_shape],
        input_output_aliases={2: 0},
        compiler_params=PARAMS,
    )(lists, counts, in_vmem(w), gather(cols, "src"))
    q = in_vmem(q)

    for sweep in range(1, ITERS):
        row_scale, cols = pl.pallas_call(
            functools.partial(col_kernel, share=total_tgt / total_src),
            in_specs=[SMEM, SMEM, VMEM, VMEM],
            out_specs=[VMEM, VMEM],
            out_shape=[row_shape, col_shape],
            scratch_shapes=[col_scratch],
            compiler_params=PARAMS,
        )(lists, counts, q, gather(rows, "tgt"))
        col_parts = gather(cols, "src")
        if sweep < ITERS - 1:
            col_scale, rows = pl.pallas_call(
                row_kernel,
                in_specs=[SMEM, SMEM, VMEM, VMEM],
                out_specs=[VMEM, VMEM],
                out_shape=[col_shape, row_shape],
                compiler_params=PARAMS,
            )(lists, counts, q, col_parts)

    col_scale, numerator, rows = pl.pallas_call(
        project_kernel,
        in_specs=[SMEM, SMEM, VMEM, VMEM, VMEM],
        out_specs=[VMEM, VMEM, VMEM],
        out_shape=[col_shape, f32(src_blocks, BLK, features), row_shape],
        compiler_params=PARAMS,
    )(lists, counts, q, col_parts, in_vmem(tgt_vmem))

    mass = lax.psum_scatter(rows, "tgt", scatter_dimension=0, tiled=True)
    share = lax.psum_scatter(numerator.reshape(src_rows, features), "tgt", tiled=True)
    mapped = share / mass.reshape(BLK, 1)

    src_square = jnp.sum(jnp.square(sources.astype(jnp.float32)), -1)
    row_potential = (
        EPSILON * (jnp.log(row_scale) - LN2 * row_lse - math.log(total_src))
    ).reshape(src_rows) + src_square / features
    col_potential = EPSILON * (
        jnp.log(col_scale) - LN2 * col_lse + (math.log(total_src) - math.log(total_tgt))
    )
    return (mapped, row_potential, col_potential.reshape(tgt_blocks * BLK))


def solution(mesh):
    in_specs = (P("src", None), P("tgt", None), P("src", "tgt", None), P("src", "tgt"))
    out_specs = (P(("src", "tgt"), None), P("src"), P("tgt"))
    return jax.shard_map(local, mesh=mesh, in_specs=in_specs, out_specs=out_specs, check_vma=False)
```

```python
import functools
import math

import jax
import jax.numpy as jnp
from jax import lax
from jax.experimental import pallas as pl
from jax.experimental.pallas import tpu as pltpu
from jax.sharding import PartitionSpec as P

BLK = 256
ITERS = 3
EPSILON = 0.1
NEGATIVE = -1e30
LOG2E = math.log2(math.e)
LN2 = math.log(2.0)
LANES = 128
SUB = 8

VMEM = pl.BlockSpec(memory_space=pltpu.VMEM)
SMEM = pl.BlockSpec(memory_space=pltpu.SMEM)
HBM = pl.BlockSpec(memory_space=pltpu.HBM)
PARAMS = pltpu.CompilerParams(vmem_limit_bytes=12 * 1024 * 1024)
NT_DIMS = (((1,), (1,)), ((), ()))


def eye():
    shape = (LANES, LANES)
    return lax.broadcasted_iota(jnp.int32, shape, 0) == lax.broadcasted_iota(jnp.int32, shape, 1)


def lane_halves(x):
    return [x[:, h : h + LANES] for h in range(0, x.shape[1], LANES)]


def to_lanes(column):
    mask = eye()
    halves = [
        jnp.sum(jnp.where(mask, column[h : h + LANES], 0.0), axis=0, keepdims=True)
        for h in range(0, BLK, LANES)
    ]
    return jnp.concatenate(halves, axis=1)


def to_sublanes(row):
    mask = eye()
    halves = [
        jnp.sum(jnp.where(mask, half, 0.0), axis=1, keepdims=True) for half in lane_halves(row)
    ]
    return jnp.concatenate(halves, axis=0)


def lane_total(x):
    halves = [
        jnp.sum(jnp.transpose(x[h : h + LANES]), axis=0, keepdims=True)
        for h in range(0, BLK, LANES)
    ]
    return jnp.concatenate(halves, axis=1)


def fold_rows(tile, op):
    parts = [tile[r : r + SUB] for r in range(0, BLK, SUB)]
    while len(parts) > 1:
        parts = [op(parts[i], parts[i + 1]) for i in range(0, len(parts), 2)]
    return parts[0]


def fold_lanes(tile, op):
    return functools.reduce(op, lane_halves(tile))


def merge_lse(values):
    peak = jnp.max(values, axis=0)
    return peak + jnp.log2(jnp.sum(jnp.exp2(values - peak[None]), axis=0))


def slot(lists, counts, b, k):
    live = k < counts[0, b]
    return jnp.where(live, lists[k, b], lists[0, b]), live


def spread(out, scratch, n):
    packed = jnp.concatenate([scratch[i, 0:1, :] for i in range(scratch.shape[0])], axis=0)
    for d in range(n):
        out[d] = packed


def cost_kernel(
    lists, counts, src_hbm, tgt_hbm, tgt, z_ref, rows, src, bias, totals, sems, *, features
):
    tgt_blocks, src_blocks, slots = tgt.shape[0], src.shape[0], z_ref.shape[1]

    def tgt_copy(t):
        return pltpu.make_async_copy(tgt_hbm.at[t], tgt.at[t], sems.at[t])

    def src_copy(b):
        return pltpu.make_async_copy(src_hbm.at[b], src.at[b], sems.at[tgt_blocks + b])

    for t in range(tgt_blocks):
        tgt_copy(t).start()
    for b in range(src_blocks):
        src_copy(b).start()
    scale = LOG2E / (features * EPSILON)

    @pl.loop(0, tgt_blocks)
    def _(t):
        tgt_copy(t).wait()
        y = tgt[t].astype(jnp.float32)
        square = fold_lanes(y * y, jnp.add)
        bias[t] = jnp.broadcast_to(-scale * lane_total(square), (SUB, BLK))

    @pl.loop(0, src_blocks)
    def _(b):
        src_copy(b).wait()
        peak = None
        for k in range(slots):
            t, live = slot(lists, counts, b, k)
            cross = lax.dot_general(src[b], tgt[t], NT_DIMS, preferred_element_type=jnp.float32)
            z = jnp.where(live, (2.0 * scale) * cross + bias[t, 0:1, :], NEGATIVE)
            z_ref[b, k] = z
            top = fold_lanes(z, jnp.maximum)
            peak = top if peak is None else jnp.maximum(peak, top)
        peak = jnp.max(peak, axis=1, keepdims=True)
        total = None
        for k in range(slots):
            part = fold_lanes(jnp.exp2(z_ref[b, k] - peak), jnp.add)
            total = part if total is None else total + part
        lse = to_lanes(peak) + jnp.log2(lane_total(total))
        totals[b] = jnp.broadcast_to(lse, (SUB, BLK))

    spread(rows, totals, rows.shape[0])


def first_col_kernel(lists, counts, z_ref, row_parts, w_ref, row_lse, cols, peaks, sums):
    src_blocks, slots, tgt_blocks = z_ref.shape[0], z_ref.shape[1], peaks.shape[0]
    row_lse[...] = merge_lse(row_parts[...])
    peaks[...] = jnp.full(peaks.shape, NEGATIVE, jnp.float32)
    sums[...] = jnp.zeros(sums.shape, jnp.float32)

    @pl.loop(0, src_blocks)
    def _(b):
        shift = to_sublanes(row_lse[pl.ds(b, 1), :])
        for k in range(slots):
            t, _ = slot(lists, counts, b, k)
            w = z_ref[b, k] - shift
            w_ref[b, k] = w
            peaks[t] = jnp.maximum(peaks[t], fold_rows(w, jnp.maximum))

    for t in range(tgt_blocks):
        peaks[t] = jnp.broadcast_to(jnp.max(peaks[t], axis=0, keepdims=True), (SUB, BLK))

    @pl.loop(0, src_blocks)
    def _(b):
        for k in range(slots):
            t, _ = slot(lists, counts, b, k)
            sums[t] += fold_rows(jnp.exp2(w_ref[b, k] - peaks[t, 0:1, :]), jnp.add)

    for t in range(tgt_blocks):
        total = jnp.sum(sums[t], axis=0, keepdims=True)
        lse = jnp.where(total > 0.0, peaks[t, 0:1, :] + jnp.log2(total), NEGATIVE)
        sums[t] = jnp.broadcast_to(lse, (SUB, BLK))
    spread(cols, sums, cols.shape[0])


def row_totals(lists, counts, tile, totals, src_blocks, slots):
    @pl.loop(0, src_blocks)
    def _(b):
        total = None
        for k in range(slots):
            t, _ = slot(lists, counts, b, k)
            part = fold_lanes(tile(b, k, t), jnp.add)
            total = part if total is None else total + part
        totals[b] = jnp.broadcast_to(lane_total(total), (SUB, BLK))


def first_row_kernel(lists, counts, w_ref, col_parts, q_ref, col_lse, rows, totals):
    col_lse[...] = merge_lse(col_parts[...])

    def tile(b, k, t):
        q = jnp.exp2(w_ref[b, k] - col_lse[pl.ds(t, 1), :])
        q_ref[b, k] = q
        return q

    row_totals(lists, counts, tile, totals, w_ref.shape[0], w_ref.shape[1])
    spread(rows, totals, rows.shape[0])


def col_kernel(lists, counts, q_ref, row_parts, row_scale, cols, sums, *, share):
    src_blocks, slots, tgt_blocks = q_ref.shape[0], q_ref.shape[1], sums.shape[0]
    row_scale[...] = share / jnp.sum(row_parts[...], axis=0)
    sums[...] = jnp.zeros(sums.shape, jnp.float32)

    @pl.loop(0, src_blocks)
    def _(b):
        scale = to_sublanes(row_scale[pl.ds(b, 1), :])
        for k in range(slots):
            t, _ = slot(lists, counts, b, k)
            sums[t] += fold_rows(q_ref[b, k] * scale, jnp.add)

    for t in range(tgt_blocks):
        sums[t] = jnp.broadcast_to(jnp.sum(sums[t], axis=0, keepdims=True), (SUB, BLK))
    spread(cols, sums, cols.shape[0])


def row_kernel(lists, counts, q_ref, col_parts, col_scale, rows, totals):
    col_scale[...] = 1.0 / jnp.sum(col_parts[...], axis=0)

    def tile(b, k, t):
        return q_ref[b, k] * col_scale[pl.ds(t, 1), :]

    row_totals(lists, counts, tile, totals, q_ref.shape[0], q_ref.shape[1])
    spread(rows, totals, rows.shape[0])


def position():
    return lax.div(lax.axis_index("tgt"), 2), lax.rem(lax.axis_index("tgt"), 2)


def block_at(step, sibling):
    chip, core = position()
    chips = lax.axis_size("tgt") // 2
    return 2 * lax.rem(chip + step + chips, chips) + (1 - core if sibling else core)


def weighted(lists, counts, q_ref, col_scale, b):
    slots = q_ref.shape[1]
    entries = [slot(lists, counts, b, k)[0] for k in range(slots)]
    return [(t, q_ref[b, k] * col_scale[pl.ds(t, 1), :]) for k, t in enumerate(entries)]


def project(weights, tgt, column, width):
    terms = [
        jnp.dot(
            w.astype(jnp.bfloat16),
            tgt[t, :, pl.ds(column, width)],
            preferred_element_type=jnp.float32,
        )
        for t, w in weights
    ]
    return functools.reduce(jnp.add, terms)


def first_project_kernel(lists, counts, q_ref, col_parts, tgt, col_scale, own, other):
    width = own.shape[2]
    col_scale[...] = 1.0 / jnp.sum(col_parts[...], axis=0)

    @pl.loop(0, 2)
    def _(i):
        column = pl.multiple_of(i * width, LANES)
        for sibling, out in ((True, other), (False, own)):
            weights = weighted(lists, counts, q_ref, col_scale, block_at(2 * i - 1, sibling))
            out[i] = project(weights, tgt, column, width)


def middle_project_kernel(lists, counts, q_ref, col_scale, tgt, own, other):
    width = own.shape[2]
    for sibling, out in ((True, other), (False, own)):
        weights = weighted(lists, counts, q_ref, col_scale, block_at(2, sibling))

        @pl.loop(0, 2)
        def _(i, out=out, weights=weights):
            out[i] = project(weights, tgt, pl.multiple_of(i * width, LANES), width)


def last_project_kernel(
    lists, counts, q_ref, col_scale, tgt, own_last, other_last, own_end, other_end, mass, totals
):
    width = own_last.shape[2]

    @pl.loop(0, 2)
    def _(i):
        column = pl.multiple_of((1 - i) * width, LANES)
        for sibling, out in ((True, other_last), (False, own_last)):
            weights = weighted(lists, counts, q_ref, col_scale, block_at(2 * i - 1, sibling))
            out[1 - i] = project(weights, tgt, column, width)

    for sibling, out in ((True, other_end), (False, own_end)):
        weights = weighted(lists, counts, q_ref, col_scale, block_at(0, sibling))

        @pl.loop(0, 2)
        def _(i, out=out, weights=weights):
            out[i] = project(weights, tgt, pl.multiple_of(i * width, LANES), width)

    def tile(b, k, t):
        return q_ref[b, k] * col_scale[pl.ds(t, 1), :]

    row_totals(lists, counts, tile, totals, q_ref.shape[0], q_ref.shape[1])
    for b in range(mass.shape[0]):
        mass[b] = totals[b, 0:1, :]


def finish_kernel(up, down, own, other, mass, out):
    width = up.shape[1]
    scale = to_sublanes(1.0 / jnp.sum(mass[...], axis=0))
    out[:, :width] = (up[...] + own[0] + other[0]) * scale
    out[:, width:] = (down[...] + own[1] + other[1]) * scale


def in_vmem(x):
    return pltpu.with_memory_space_constraint(x, pltpu.VMEM)


def in_hbm(x):
    return pltpu.with_memory_space_constraint(x, pltpu.HBM)


def f32(*shape):
    return jax.ShapeDtypeStruct(shape, jnp.float32)


def v32(*shape):
    return pltpu.VMEM(shape, jnp.float32)


def exchange(copies, axis):
    return in_vmem(lax.all_to_all(copies, axis, 0, 0))


def local(sources, targets, block_lists, live_counts):
    src_rows, features = sources.shape
    src_blocks = src_rows // BLK
    tgt_blocks = targets.shape[0] // BLK
    slots = block_lists.shape[2]
    n_src, n_tgt = lax.axis_size("src"), lax.axis_size("tgt")
    total_src = src_rows * n_src
    total_tgt = targets.shape[0] * n_tgt
    src_blocked = sources.reshape(src_blocks, BLK, features)
    tgt_blocked = targets.reshape(tgt_blocks, BLK, features)
    lists = (block_lists[:, 0, :].T, live_counts.T)
    tiles = v32(src_blocks, slots, BLK, BLK)
    row_shape, col_shape = f32(src_blocks, BLK), f32(tgt_blocks, BLK)
    row_sends, col_sends = v32(n_tgt, src_blocks, BLK), v32(n_src, tgt_blocks, BLK)
    row_scratch, col_scratch = v32(src_blocks, SUB, BLK), v32(tgt_blocks, SUB, BLK)

    tgt_vmem, z, rows = pl.pallas_call(
        functools.partial(cost_kernel, features=features),
        in_specs=[SMEM, SMEM, HBM, HBM],
        out_specs=[VMEM, VMEM, VMEM],
        out_shape=[pltpu.VMEM(tgt_blocked.shape, jnp.bfloat16), tiles, row_sends],
        scratch_shapes=[
            pltpu.VMEM(src_blocked.shape, jnp.bfloat16),
            col_scratch,
            row_scratch,
            pltpu.SemaphoreType.DMA((tgt_blocks + src_blocks,)),
        ],
        compiler_params=PARAMS,
        name="cost",
    )(*lists, in_hbm(src_blocked), in_hbm(tgt_blocked))

    w, row_lse, cols = pl.pallas_call(
        first_col_kernel,
        in_specs=[SMEM, SMEM, VMEM, VMEM],
        out_specs=[VMEM, VMEM, VMEM],
        out_shape=[tiles, row_shape, col_sends],
        scratch_shapes=[col_scratch, col_scratch],
        input_output_aliases={2: 0},
        compiler_params=PARAMS,
        name="first_col",
    )(*lists, in_vmem(z), exchange(rows, "tgt"))

    q, col_lse, rows = pl.pallas_call(
        first_row_kernel,
        in_specs=[SMEM, SMEM, VMEM, VMEM],
        out_specs=[VMEM, VMEM, VMEM],
        out_shape=[tiles, col_shape, row_sends],
        scratch_shapes=[row_scratch],
        input_output_aliases={2: 0},
        compiler_params=PARAMS,
        name="first_row",
    )(*lists, in_vmem(w), exchange(cols, "src"))
    q = in_vmem(q)

    for sweep in range(1, ITERS):
        row_scale, cols = pl.pallas_call(
            functools.partial(col_kernel, share=total_tgt / total_src),
            in_specs=[SMEM, SMEM, VMEM, VMEM],
            out_specs=[VMEM, VMEM],
            out_shape=[row_shape, col_sends],
            scratch_shapes=[col_scratch],
            compiler_params=PARAMS,
            name="col_sums",
        )(*lists, q, exchange(rows, "tgt"))
        col_parts = exchange(cols, "src")
        if sweep < ITERS - 1:
            col_scale, rows = pl.pallas_call(
                row_kernel,
                in_specs=[SMEM, SMEM, VMEM, VMEM],
                out_specs=[VMEM, VMEM],
                out_shape=[col_shape, row_sends],
                scratch_shapes=[row_scratch],
                compiler_params=PARAMS,
                name="row_sums",
            )(*lists, q, col_parts)

    chips = n_tgt // 2
    tgt_vmem = in_vmem(tgt_vmem)
    half = v32(2, BLK, features // 2)

    def swap(x):
        return lax.ppermute(x, "tgt", [(t, t ^ 1) for t in range(n_tgt)])

    def along(x, step):
        pairs = [(t, 2 * ((t // 2 + step) % chips) + t % 2) for t in range(n_tgt)]
        return lax.ppermute(x, "tgt", pairs)

    col_scale, own, other = pl.pallas_call(
        first_project_kernel,
        in_specs=[SMEM, SMEM, VMEM, VMEM, VMEM],
        out_specs=[VMEM] * 3,
        out_shape=[col_shape, half, half],
        compiler_params=PARAMS,
        name="project_first",
    )(*lists, q, col_parts, tgt_vmem)
    first = own + swap(other)
    own_middle, other_middle = pl.pallas_call(
        middle_project_kernel,
        in_specs=[SMEM, SMEM, VMEM, VMEM, VMEM],
        out_specs=[VMEM] * 2,
        out_shape=[half] * 2,
        compiler_params=PARAMS,
        name="project_middle",
    )(*lists, q, col_scale, tgt_vmem)
    up, down = along(first[0], 1), along(first[1], -1)
    first, col_scale = lax.optimization_barrier((first, col_scale))
    own_last, other_last, own_end, other_end, mass = pl.pallas_call(
        last_project_kernel,
        in_specs=[SMEM, SMEM, VMEM, VMEM, VMEM],
        out_specs=[VMEM] * 5,
        out_shape=[half] * 4 + [v32(src_blocks, 1, BLK)],
        scratch_shapes=[row_scratch],
        compiler_params=PARAMS,
        name="project_last",
    )(*lists, q, col_scale, tgt_vmem)
    middle = own_middle + swap(other_middle)
    up, down = along(up + middle[0], 1), along(down + middle[1], -1)
    last = own_last + swap(other_last)
    up, down = along(up + last[0], 1), along(down + last[1], -1)
    mapped = pl.pallas_call(
        finish_kernel,
        in_specs=[VMEM] * 5,
        out_specs=VMEM,
        out_shape=f32(BLK, features),
        compiler_params=PARAMS,
        name="finish",
    )(up, down, own_end, swap(other_end), lax.all_to_all(mass, "tgt", 0, 0))

    src_square = jnp.sum(jnp.square(sources.astype(jnp.float32)), -1)
    row_potential = (
        EPSILON * (jnp.log(row_scale) - LN2 * row_lse - math.log(total_src))
    ).reshape(src_rows) + src_square / features
    col_potential = EPSILON * (
        jnp.log(col_scale) - LN2 * col_lse + (math.log(total_src) - math.log(total_tgt))
    )
    return (mapped, row_potential, col_potential.reshape(tgt_blocks * BLK))


def solution(mesh):
    in_specs = (P("src", None), P("tgt", None), P("src", "tgt", None), P("src", "tgt"))
    out_specs = (P(("src", "tgt"), None), P("src"), P("tgt"))
    return jax.shard_map(local, mesh=mesh, in_specs=in_specs, out_specs=out_specs, check_vma=False)
```

```python
import functools
import math

import jax
import jax.numpy as jnp
from jax import lax
from jax.experimental import pallas as pl
from jax.experimental.pallas import tpu as pltpu
from jax.sharding import Mesh
from jax.sharding import PartitionSpec as P

BLK = 256
ITERS = 3
EPSILON = 0.1
NEGATIVE = -1e30
LOG2E = math.log2(math.e)
LN2 = math.log(2.0)
LANES = 128
SUB = 8
GROUP = 8
CHIPS_X = 4
SRC = ("z", "x")

VMEM = pl.BlockSpec(memory_space=pltpu.VMEM)
SMEM = pl.BlockSpec(memory_space=pltpu.SMEM)
HBM = pl.BlockSpec(memory_space=pltpu.HBM)
PARAMS = pltpu.CompilerParams(vmem_limit_bytes=12 * 1024 * 1024)
NT_DIMS = (((1,), (1,)), ((), ()))


def eye():
    shape = (LANES, LANES)
    return lax.broadcasted_iota(jnp.int32, shape, 0) == lax.broadcasted_iota(jnp.int32, shape, 1)


def lane_halves(x):
    return [x[:, h : h + LANES] for h in range(0, x.shape[1], LANES)]


def to_lanes(column):
    mask = eye()
    halves = [
        jnp.sum(jnp.where(mask, column[h : h + LANES], 0.0), axis=0, keepdims=True)
        for h in range(0, BLK, LANES)
    ]
    return jnp.concatenate(halves, axis=1)


def to_sublanes(row):
    mask = eye()
    halves = [
        jnp.sum(jnp.where(mask, half, 0.0), axis=1, keepdims=True) for half in lane_halves(row)
    ]
    return jnp.concatenate(halves, axis=0)


def along_rows(row):
    halves = [
        jnp.transpose(jnp.broadcast_to(half, (LANES, LANES))) for half in lane_halves(row)
    ]
    column = jnp.concatenate(halves, axis=0)
    return jnp.concatenate([column] * (BLK // LANES), axis=1)


def lane_total(x):
    halves = [
        jnp.sum(jnp.transpose(x[h : h + LANES]), axis=0, keepdims=True)
        for h in range(0, BLK, LANES)
    ]
    return jnp.concatenate(halves, axis=1)


def fold_rows(tile, op):
    parts = [tile[r : r + SUB] for r in range(0, BLK, SUB)]
    while len(parts) > 1:
        parts = [op(parts[i], parts[i + 1]) for i in range(0, len(parts), 2)]
    return parts[0]


def fold_lanes(tile, op):
    return functools.reduce(op, lane_halves(tile))


def merge_lse(values):
    peak = jnp.max(values, axis=0)
    return peak + jnp.log2(jnp.sum(jnp.exp2(values - peak[None]), axis=0))


def spread(out, scratch, n):
    packed = jnp.concatenate([scratch[i, 0:1, :] for i in range(scratch.shape[0])], axis=0)
    for d in range(n):
        out[d] = packed


def cost_kernel(
    lists_hbm, counts_hbm, src_hbm, tgt_hbm,
    tgt, z_ref, rows, table,
    lists, counts, order, place, src, bias, totals, sems, list_sems,
    *, features,
):
    tgt_blocks, src_blocks, slots = tgt.shape[0], src.shape[0], z_ref.shape[1]
    share = tgt_blocks * GROUP // (src_blocks * slots)
    list_copies = [
        pltpu.make_async_copy(lists_hbm, lists, list_sems.at[0]),
        pltpu.make_async_copy(counts_hbm, counts, list_sems.at[1]),
    ]

    def tgt_copy(t):
        return pltpu.make_async_copy(tgt_hbm.at[t], tgt.at[t], sems.at[t])

    def src_copy(b):
        return pltpu.make_async_copy(src_hbm.at[b], src.at[b], sems.at[tgt_blocks + b])

    for copy in list_copies:
        copy.start()
    for b in range(src_blocks):
        src_copy(b).start()
    for t in range(tgt_blocks):
        tgt_copy(t).start()
    for copy in list_copies:
        copy.wait()

    for t in range(tgt_blocks):
        place[t] = 0
    for b in range(src_blocks):
        for k in range(slots):
            t = jnp.where(k < counts[0, b], lists[k, b], lists[0, b])
            table[b * slots + k] = t
            place[t] = place[t] + 1
    start = 0
    for t in range(tgt_blocks):
        count = place[t]
        place[t] = start
        start = start + count
    for n in range(src_blocks * slots):
        t = table[n]
        order[place[t]] = n
        place[t] = place[t] + 1

    for b in range(src_blocks):
        src_copy(b).wait()
    scale = LOG2E / (features * EPSILON)

    def arrived(t, carry):
        tgt_copy(t).wait()
        return carry

    def cross_terms(g, ready):
        entries = [order[g * GROUP + i] for i in range(GROUP)]
        blocks = [table[n] for n in entries]
        squares = [g * share + i for i in range(share)]
        needed = jnp.maximum(ready, jnp.maximum(squares[-1], blocks[-1]) + 1)
        lax.fori_loop(ready, needed, arrived, 0)
        for n, block in zip(entries, blocks):
            z_ref[n // slots, n % slots] = lax.dot_general(
                src[n // slots], tgt[block], NT_DIMS, preferred_element_type=jnp.float32
            )
        for t in squares:
            y = tgt[t].astype(jnp.float32)
            square = fold_lanes(y * y, jnp.add)
            bias[t] = jnp.broadcast_to(-scale * lane_total(square), (SUB, BLK))
        return needed

    lax.fori_loop(0, src_blocks * slots // GROUP, cross_terms, 0)

    @pl.loop(0, src_blocks, unroll=2)
    def _(b):
        peak = None
        for k in range(slots):
            live = k < counts[0, b]
            offset = jnp.where(live, bias[table[b * slots + k], 0:1, :], NEGATIVE)
            z = (2.0 * scale) * z_ref[b, k] + offset
            z_ref[b, k] = z
            top = fold_lanes(z, jnp.maximum)
            peak = top if peak is None else jnp.maximum(peak, top)
        peak = jnp.max(peak, axis=1, keepdims=True)
        total = None
        for k in range(slots):
            part = fold_lanes(jnp.exp2(z_ref[b, k] - peak), jnp.add)
            total = part if total is None else total + part
        lse = to_lanes(peak) + jnp.log2(lane_total(total))
        totals[b] = jnp.broadcast_to(lse, (SUB, BLK))

    spread(rows, totals, rows.shape[0])


def first_col_kernel(table, z_ref, row_parts, w_ref, row_lse, cols, peaks, sums):
    src_blocks, slots, tgt_blocks = z_ref.shape[0], z_ref.shape[1], peaks.shape[0]
    row_lse[...] = merge_lse(row_parts[...])
    peaks[...] = jnp.full(peaks.shape, NEGATIVE, jnp.float32)
    sums[...] = jnp.zeros(sums.shape, jnp.float32)

    @pl.loop(0, src_blocks)
    def _(b):
        shift = along_rows(row_lse[pl.ds(b, 1), :])
        for k in range(slots):
            t = table[b * slots + k]
            w = z_ref[b, k] - shift
            w_ref[b, k] = w
            top = jnp.max(fold_rows(w, jnp.maximum), axis=0, keepdims=True)
            total = fold_rows(jnp.exp2(w - top), jnp.add)
            old = peaks[t]
            new = jnp.maximum(old, top)
            peaks[t] = new
            sums[t] = sums[t] * jnp.exp2(old - new) + total * jnp.exp2(top - new)

    for t in range(tgt_blocks):
        total = jnp.sum(sums[t], axis=0, keepdims=True)
        lse = jnp.where(total > 0.0, peaks[t, 0:1, :] + jnp.log2(total), NEGATIVE)
        sums[t] = jnp.broadcast_to(lse, (SUB, BLK))
    spread(cols, sums, cols.shape[0])


def row_totals(table, tile, totals, src_blocks, slots):
    @pl.loop(0, src_blocks)
    def _(b):
        total = None
        for k in range(slots):
            t = table[b * slots + k]
            part = fold_lanes(tile(b, k, t), jnp.add)
            total = part if total is None else total + part
        totals[b] = jnp.broadcast_to(lane_total(total), (SUB, BLK))


def first_row_kernel(table, w_ref, col_parts, q_ref, col_lse, rows, totals):
    col_lse[...] = merge_lse(col_parts[...])

    def tile(b, k, t):
        q = jnp.exp2(w_ref[b, k] - col_lse[pl.ds(t, 1), :])
        q_ref[b, k] = q
        return q

    row_totals(table, tile, totals, w_ref.shape[0], w_ref.shape[1])
    spread(rows, totals, rows.shape[0])


def col_kernel(table, q_ref, row_parts, row_scale, cols, sums, *, share):
    src_blocks, slots, tgt_blocks = q_ref.shape[0], q_ref.shape[1], sums.shape[0]
    row_scale[...] = share / jnp.sum(row_parts[...], axis=0)
    sums[...] = jnp.zeros(sums.shape, jnp.float32)

    @pl.loop(0, src_blocks)
    def _(b):
        scale = along_rows(row_scale[pl.ds(b, 1), :])
        for k in range(slots):
            t = table[b * slots + k]
            sums[t] += fold_rows(q_ref[b, k] * scale, jnp.add)

    for t in range(tgt_blocks):
        sums[t] = jnp.broadcast_to(jnp.sum(sums[t], axis=0, keepdims=True), (SUB, BLK))
    spread(cols, sums, cols.shape[0])


def row_kernel(table, q_ref, col_parts, col_scale, rows, totals):
    col_scale[...] = 1.0 / jnp.sum(col_parts[...], axis=0)

    def tile(b, k, t):
        return q_ref[b, k] * col_scale[pl.ds(t, 1), :]

    row_totals(table, tile, totals, q_ref.shape[0], q_ref.shape[1])
    spread(rows, totals, rows.shape[0])


def block_at(flip, sibling):
    chip, core = lax.div(lax.axis_index("tgt"), 2), lax.rem(lax.axis_index("tgt"), 2)
    return 2 * lax.bitwise_xor(chip, flip) + (1 - core if sibling else core)


def weighted(table, q_ref, col_scale, b):
    slots = q_ref.shape[1]
    entries = [table[b * slots + k] for k in range(slots)]
    return [(t, q_ref[b, k] * col_scale[pl.ds(t, 1), :]) for k, t in enumerate(entries)]


def project(table, q_ref, col_scale, tgt, block, outs, width):
    weights = weighted(table, q_ref, col_scale, block)
    rows = [(t, w.astype(jnp.bfloat16)) for t, w in weights]
    total = functools.reduce(jnp.add, [fold_lanes(w, jnp.add) for _, w in weights])
    mass = jnp.broadcast_to(lane_total(total), (SUB, BLK))
    for n, out in enumerate(outs):
        columns = slice(n * width, (n + 1) * width)
        terms = [
            jnp.dot(w, tgt[t, :, columns], preferred_element_type=jnp.float32) for t, w in rows
        ]
        out[:BLK, :] = functools.reduce(jnp.add, terms)
        out[BLK:, :BLK] = mass
        out[BLK:, BLK:] = jnp.zeros((SUB, width - BLK), jnp.float32)


def far_kernel(table, q_ref, col_parts, tgt, col_scale, own, other):
    col_scale[...] = 1.0 / jnp.sum(col_parts[...], axis=0)
    for sibling, out in ((True, other), (False, own)):
        halves = [out.at[0], out.at[1]]
        project(table, q_ref, col_scale, tgt, block_at(2, sibling), halves, out.shape[2])


def side_kernel(table, q_ref, col_scale, tgt, own, other):
    @pl.loop(0, 2)
    def _(i):
        for sibling, out in ((True, other), (False, own)):
            block = block_at(2 * i + 1, sibling)
            project(table, q_ref, col_scale, tgt, block, [out.at[i]], out.shape[2])


def end_kernel(table, q_ref, col_scale, tgt, own, other):
    for sibling, out in ((True, other), (False, own)):
        project(table, q_ref, col_scale, tgt, block_at(0, sibling), [out], out.shape[1])


def far_sum_kernel(own, other, low, high):
    low[...] = own[0] + other[0]
    high[...] = own[1] + other[1]


def side_sum_kernel(own, other, low, high, first, second):
    width = low.shape[1]
    first[:, :width] = own[0, :, :width] + other[0, :, :width]
    first[:, width:] = own[0, :, width:] + other[0, :, width:] + high[...]
    second[:, :width] = own[1, :, :width] + other[1, :, :width] + low[...]
    second[:, width:] = own[1, :, width:] + other[1, :, width:]


def finish_kernel(first, second, own, other, out):
    mass = (first[BLK:] + second[BLK:] + own[BLK:] + other[BLK:])[0:1, :BLK]
    total = first[:BLK] + second[:BLK] + own[:BLK] + other[:BLK]
    out[...] = total * to_sublanes(1.0 / mass)


def in_vmem(x):
    return pltpu.with_memory_space_constraint(x, pltpu.VMEM)


def in_hbm(x):
    return pltpu.with_memory_space_constraint(x, pltpu.HBM)


def f32(*shape):
    return jax.ShapeDtypeStruct(shape, jnp.float32)


def v32(*shape):
    return pltpu.VMEM(shape, jnp.float32)


def exchange(copies, axis):
    return in_vmem(lax.all_to_all(copies, axis, 0, 0))


def add_parts(values):
    return jnp.sum(values, axis=0)


def merge_kernel(merge, parts, tiles, out, kept):
    merged = merge(parts[...])
    for d in range(out.shape[0]):
        out[d] = merged


def exchange_cols(copies, merge, tiles):
    parts = exchange(copies, "z")
    sends, tiles = pl.pallas_call(
        functools.partial(merge_kernel, merge),
        in_specs=[VMEM] * 2,
        out_specs=[VMEM] * 2,
        out_shape=[
            v32(lax.axis_size("x"), *parts.shape[1:]),
            pltpu.VMEM(tiles.shape, jnp.float32),
        ],
        input_output_aliases={1: 1},
        compiler_params=PARAMS,
        name="merge",
    )(parts, tiles)
    return exchange(sends, "x"), in_vmem(tiles)


def local(sources, targets, block_lists, live_counts):
    src_rows, features = sources.shape
    src_blocks = src_rows // BLK
    tgt_blocks = targets.shape[0] // BLK
    slots = block_lists.shape[2]
    n_z, n_x, n_tgt = (lax.axis_size(a) for a in ("z", "x", "tgt"))
    total_src = src_rows * n_z * n_x
    total_tgt = targets.shape[0] * n_tgt
    src_blocked = sources.reshape(src_blocks, BLK, features)
    tgt_blocked = targets.reshape(tgt_blocks, BLK, features)
    lists = (block_lists[:, 0, :].T, live_counts.T)
    tiles = v32(src_blocks, slots, BLK, BLK)
    row_shape, col_shape = v32(src_blocks, BLK), v32(tgt_blocks, BLK)
    row_sends, col_sends = v32(n_tgt, src_blocks, BLK), v32(n_z, tgt_blocks, BLK)
    row_scratch, col_scratch = v32(src_blocks, SUB, BLK), v32(tgt_blocks, SUB, BLK)

    tgt_vmem, z, rows, table = pl.pallas_call(
        functools.partial(cost_kernel, features=features),
        in_specs=[HBM] * 4,
        out_specs=[VMEM, VMEM, VMEM, SMEM],
        out_shape=[
            pltpu.VMEM(tgt_blocked.shape, jnp.bfloat16),
            tiles,
            row_sends,
            pltpu.SMEM((src_blocks * slots,), jnp.int32),
        ],
        scratch_shapes=[
            pltpu.SMEM((slots, src_blocks), jnp.int32),
            pltpu.SMEM((1, src_blocks), jnp.int32),
            pltpu.SMEM((src_blocks * slots,), jnp.int32),
            pltpu.SMEM((tgt_blocks,), jnp.int32),
            pltpu.VMEM(src_blocked.shape, jnp.bfloat16),
            col_scratch,
            row_scratch,
            pltpu.SemaphoreType.DMA((tgt_blocks + src_blocks,)),
            pltpu.SemaphoreType.DMA((2,)),
        ],
        compiler_params=PARAMS,
        name="cost",
    )(*[in_hbm(x) for x in (*lists, src_blocked, tgt_blocked)])
    table = pltpu.with_memory_space_constraint(table, pltpu.SMEM)

    w, row_lse, cols = pl.pallas_call(
        first_col_kernel,
        in_specs=[SMEM, VMEM, VMEM],
        out_specs=[VMEM, VMEM, VMEM],
        out_shape=[tiles, f32(src_blocks, BLK), col_sends],
        scratch_shapes=[col_scratch, col_scratch],
        input_output_aliases={1: 0},
        compiler_params=PARAMS,
        name="first_col",
    )(table, in_vmem(z), exchange(rows, "tgt"))

    col_parts, w = exchange_cols(cols, merge_lse, in_vmem(w))
    q, col_lse, rows = pl.pallas_call(
        first_row_kernel,
        in_specs=[SMEM, VMEM, VMEM],
        out_specs=[VMEM, VMEM, VMEM],
        out_shape=[tiles, f32(tgt_blocks, BLK), row_sends],
        scratch_shapes=[row_scratch],
        input_output_aliases={1: 0},
        compiler_params=PARAMS,
        name="first_row",
    )(table, w, col_parts)
    q = in_vmem(q)

    for sweep in range(1, ITERS):
        row_scale, cols = pl.pallas_call(
            functools.partial(col_kernel, share=total_tgt / total_src),
            in_specs=[SMEM, VMEM, VMEM],
            out_specs=[VMEM, VMEM],
            out_shape=[row_shape, col_sends],
            scratch_shapes=[col_scratch],
            compiler_params=PARAMS,
            name="col_sums",
        )(table, q, exchange(rows, "tgt"))
        col_parts, q = exchange_cols(cols, add_parts, q)
        if sweep < ITERS - 1:
            col_scale, rows = pl.pallas_call(
                row_kernel,
                in_specs=[SMEM, VMEM, VMEM],
                out_specs=[VMEM, VMEM],
                out_shape=[col_shape, row_sends],
                scratch_shapes=[row_scratch],
                compiler_params=PARAMS,
                name="row_sums",
            )(table, q, col_parts)

    tgt_vmem = in_vmem(tgt_vmem)
    block = v32(BLK + SUB, features)
    blocks = v32(2, BLK + SUB, features)
    halves = v32(2, BLK + SUB, features // 2)
    half = v32(BLK + SUB, features // 2)

    def swap(x, flip=1):
        return in_vmem(lax.ppermute(x, "tgt", [(t, t ^ flip) for t in range(n_tgt)]))

    def call(kernel, name, operands, out_shape, spec=VMEM):
        return pl.pallas_call(
            kernel,
            in_specs=[spec] + [VMEM] * (len(operands) - 1),
            out_specs=[VMEM] * len(out_shape),
            out_shape=out_shape,
            compiler_params=PARAMS,
            name=name,
        )(*operands)

    col_scale, own_far, other_far = call(
        far_kernel, "far", [table, q, col_parts, tgt_vmem], [col_shape, halves, halves], SMEM
    )
    low, high = call(
        far_sum_kernel, "far_sum", [in_vmem(own_far), swap(other_far)], [half, half]
    )
    (low, high), col_scale = lax.optimization_barrier(((low, high), col_scale))
    low, high = swap(low, 2), swap(high, 6)
    own_side, other_side = call(
        side_kernel, "side", [table, q, in_vmem(col_scale), tgt_vmem], [blocks, blocks], SMEM
    )
    own_side, col_scale = lax.optimization_barrier((own_side, col_scale))
    own_end, other_end = call(
        end_kernel, "end", [table, q, in_vmem(col_scale), tgt_vmem], [block, block], SMEM
    )
    first, second = call(
        side_sum_kernel,
        "side_sum",
        [in_vmem(own_side), swap(other_side), low, high],
        [block, block],
    )
    mapped = call(
        finish_kernel,
        "finish",
        [swap(first, 2), swap(second, 6), in_vmem(own_end), swap(other_end)],
        [f32(BLK, features)],
    )[0]

    src_square = jnp.sum(jnp.square(sources.astype(jnp.float32)), -1)
    row_potential = (
        EPSILON * (jnp.log(row_scale) - LN2 * row_lse - math.log(total_src))
    ).reshape(src_rows) + src_square / features
    col_potential = EPSILON * (
        jnp.log(col_scale) - LN2 * col_lse + (math.log(total_src) - math.log(total_tgt))
    )
    return (mapped, row_potential, col_potential.reshape(tgt_blocks * BLK))


def solution(mesh):
    n_src, n_tgt = mesh.shape["src"], mesh.shape["tgt"]
    grid = Mesh(mesh.devices.reshape(n_src // CHIPS_X, CHIPS_X, n_tgt), ("z", "x", "tgt"))
    in_specs = (P(SRC, None), P("tgt", None), P(SRC, "tgt", None), P(SRC, "tgt"))
    out_specs = (P((*SRC, "tgt"), None), P(SRC), P("tgt"))
    return jax.shard_map(local, mesh=grid, in_specs=in_specs, out_specs=out_specs, check_vma=False)
```

```python
import functools
import math

import jax
import jax.numpy as jnp
from jax import lax
from jax.experimental import pallas as pl
from jax.experimental.pallas import tpu as pltpu
from jax.sharding import Mesh
from jax.sharding import PartitionSpec as P

BLK = 256
ITERS = 3
EPSILON = 0.1
NEGATIVE = -1e30
LOG2E = math.log2(math.e)
LN2 = math.log(2.0)
LANES = 128
SUB = 8
GROUP = 8
X_HALVES = 2
X_AXES = ("x_high", "x_low")
SRC = ("z", *X_AXES)
GATHER = ("z", "x_low")

VMEM = pl.BlockSpec(memory_space=pltpu.VMEM)
SMEM = pl.BlockSpec(memory_space=pltpu.SMEM)
HBM = pl.BlockSpec(memory_space=pltpu.HBM)
PARAMS = pltpu.CompilerParams(vmem_limit_bytes=12 * 1024 * 1024)
NT_DIMS = (((1,), (1,)), ((), ()))


def eye():
    shape = (LANES, LANES)
    return lax.broadcasted_iota(jnp.int32, shape, 0) == lax.broadcasted_iota(jnp.int32, shape, 1)


def lane_halves(x):
    return [x[:, h : h + LANES] for h in range(0, x.shape[1], LANES)]


def to_lanes(column):
    mask = eye()
    halves = [
        jnp.sum(jnp.where(mask, column[h : h + LANES], 0.0), axis=0, keepdims=True)
        for h in range(0, BLK, LANES)
    ]
    return jnp.concatenate(halves, axis=1)


def to_sublanes(row):
    mask = eye()
    halves = [
        jnp.sum(jnp.where(mask, half, 0.0), axis=1, keepdims=True) for half in lane_halves(row)
    ]
    return jnp.concatenate(halves, axis=0)


def along_rows(row):
    halves = [
        jnp.transpose(jnp.broadcast_to(half, (LANES, LANES))) for half in lane_halves(row)
    ]
    column = jnp.concatenate(halves, axis=0)
    return jnp.concatenate([column] * (BLK // LANES), axis=1)


def lane_total(x):
    halves = [
        jnp.sum(jnp.transpose(x[h : h + LANES]), axis=0, keepdims=True)
        for h in range(0, BLK, LANES)
    ]
    return jnp.concatenate(halves, axis=1)


def fold_rows(tile, op):
    parts = [tile[r : r + SUB] for r in range(0, BLK, SUB)]
    while len(parts) > 1:
        parts = [op(parts[i], parts[i + 1]) for i in range(0, len(parts), 2)]
    return parts[0]


def fold_lanes(tile, op):
    return functools.reduce(op, lane_halves(tile))


def add_parts(values):
    pairs = [values[i] + values[i + 1] for i in range(0, values.shape[0], 2)]
    return functools.reduce(jnp.add, pairs)


def merge_lse(values):
    peak = jnp.max(values, axis=0)
    return peak + jnp.log2(add_parts(jnp.exp2(values - peak[None])))


def spread(out, scratch, n):
    packed = jnp.concatenate([scratch[i, 0:1, :] for i in range(scratch.shape[0])], axis=0)
    for d in range(n):
        out[d] = packed


def cost_kernel(
    lists_hbm, counts_hbm, src_hbm, tgt_hbm,
    tgt, z_ref, rows, table,
    lists, counts, order, place, src, bias, totals, sems, list_sems,
    *, features,
):
    tgt_blocks, src_blocks, slots = tgt.shape[0], src.shape[0], z_ref.shape[1]
    share = tgt_blocks * GROUP // (src_blocks * slots)
    list_copies = [
        pltpu.make_async_copy(lists_hbm, lists, list_sems.at[0]),
        pltpu.make_async_copy(counts_hbm, counts, list_sems.at[1]),
    ]

    def tgt_copy(t):
        return pltpu.make_async_copy(tgt_hbm.at[t], tgt.at[t], sems.at[t])

    def src_copy(b):
        return pltpu.make_async_copy(src_hbm.at[b], src.at[b], sems.at[tgt_blocks + b])

    for copy in list_copies:
        copy.start()
    for b in range(src_blocks):
        src_copy(b).start()
    for t in range(tgt_blocks):
        tgt_copy(t).start()
    for copy in list_copies:
        copy.wait()

    for t in range(tgt_blocks):
        place[t] = 0
    for b in range(src_blocks):
        for k in range(slots):
            t = jnp.where(k < counts[0, b], lists[k, b], lists[0, b])
            table[b * slots + k] = t
            place[t] = place[t] + 1
    start = 0
    for t in range(tgt_blocks):
        count = place[t]
        place[t] = start
        start = start + count
    for n in range(src_blocks * slots):
        t = table[n]
        order[place[t]] = n
        place[t] = place[t] + 1

    for b in range(src_blocks):
        src_copy(b).wait()
    scale = LOG2E / (features * EPSILON)

    def arrived(t, carry):
        tgt_copy(t).wait()
        return carry

    def cross_terms(g, ready):
        entries = [order[g * GROUP + i] for i in range(GROUP)]
        blocks = [table[n] for n in entries]
        squares = [g * share + i for i in range(share)]
        needed = jnp.maximum(ready, jnp.maximum(squares[-1], blocks[-1]) + 1)
        lax.fori_loop(ready, needed, arrived, 0)
        for n, block in zip(entries, blocks):
            z_ref[n // slots, n % slots] = lax.dot_general(
                src[n // slots], tgt[block], NT_DIMS, preferred_element_type=jnp.float32
            )
        for t in squares:
            y = tgt[t].astype(jnp.float32)
            square = fold_lanes(y * y, jnp.add)
            bias[t] = jnp.broadcast_to(-scale * lane_total(square), (SUB, BLK))
        return needed

    lax.fori_loop(0, src_blocks * slots // GROUP, cross_terms, 0)

    @pl.loop(0, src_blocks, unroll=4)
    def _(b):
        peak = None
        for k in range(slots):
            live = k < counts[0, b]
            offset = jnp.where(live, bias[table[b * slots + k], 0:1, :], NEGATIVE)
            z = (2.0 * scale) * z_ref[b, k] + offset
            z_ref[b, k] = z
            top = fold_lanes(z, jnp.maximum)
            peak = top if peak is None else jnp.maximum(peak, top)
        peak = jnp.max(peak, axis=1, keepdims=True)
        total = None
        for k in range(slots):
            part = fold_lanes(jnp.exp2(z_ref[b, k] - peak), jnp.add)
            total = part if total is None else total + part
        lse = to_lanes(peak) + jnp.log2(lane_total(total))
        totals[b] = jnp.broadcast_to(lse, (SUB, BLK))

    spread(rows, totals, rows.shape[0])


def first_col_kernel(table, z_ref, row_parts, w_ref, row_lse, cols, peaks, sums):
    src_blocks, slots, tgt_blocks = z_ref.shape[0], z_ref.shape[1], peaks.shape[0]
    row_lse[...] = merge_lse(row_parts[...])
    peaks[...] = jnp.full(peaks.shape, NEGATIVE, jnp.float32)
    sums[...] = jnp.zeros(sums.shape, jnp.float32)

    @pl.loop(0, src_blocks)
    def _(b):
        shift = along_rows(row_lse[pl.ds(b, 1), :])
        for k in range(slots):
            t = table[b * slots + k]
            w = z_ref[b, k] - shift
            w_ref[b, k] = w
            top = jnp.max(fold_rows(w, jnp.maximum), axis=0, keepdims=True)
            total = fold_rows(jnp.exp2(w - top), jnp.add)
            old = peaks[t]
            new = jnp.maximum(old, top)
            peaks[t] = new
            sums[t] = sums[t] * jnp.exp2(old - new) + total * jnp.exp2(top - new)

    for t in range(tgt_blocks):
        total = jnp.sum(sums[t], axis=0, keepdims=True)
        lse = jnp.where(total > 0.0, peaks[t, 0:1, :] + jnp.log2(total), NEGATIVE)
        sums[t] = jnp.broadcast_to(lse, (SUB, BLK))
    spread(cols, sums, cols.shape[0])


def row_totals(table, tile, totals, src_blocks, slots):
    @pl.loop(0, src_blocks)
    def _(b):
        total = None
        for k in range(slots):
            t = table[b * slots + k]
            part = fold_lanes(tile(b, k, t), jnp.add)
            total = part if total is None else total + part
        totals[b] = jnp.broadcast_to(lane_total(total), (SUB, BLK))


def first_row_kernel(table, w_ref, col_parts, q_ref, col_lse, rows, totals):
    col_lse[...] = merge_lse(col_parts[...])

    def tile(b, k, t):
        q = jnp.exp2(w_ref[b, k] - col_lse[pl.ds(t, 1), :])
        q_ref[b, k] = q
        return q

    row_totals(table, tile, totals, w_ref.shape[0], w_ref.shape[1])
    spread(rows, totals, rows.shape[0])


def col_kernel(table, q_ref, row_parts, row_scale, cols, sums, *, share):
    src_blocks, slots, tgt_blocks = q_ref.shape[0], q_ref.shape[1], sums.shape[0]
    row_scale[...] = share / add_parts(row_parts[...])
    sums[...] = jnp.zeros(sums.shape, jnp.float32)

    @pl.loop(0, src_blocks)
    def _(b):
        scale = along_rows(row_scale[pl.ds(b, 1), :])
        for k in range(slots):
            t = table[b * slots + k]
            sums[t] += fold_rows(q_ref[b, k] * scale, jnp.add)

    for t in range(tgt_blocks):
        sums[t] = jnp.broadcast_to(jnp.sum(sums[t], axis=0, keepdims=True), (SUB, BLK))
    spread(cols, sums, cols.shape[0])


def row_kernel(table, q_ref, col_parts, col_scale, rows, totals):
    col_scale[...] = 1.0 / add_parts(col_parts[...])

    def tile(b, k, t):
        return q_ref[b, k] * col_scale[pl.ds(t, 1), :]

    row_totals(table, tile, totals, q_ref.shape[0], q_ref.shape[1])
    spread(rows, totals, rows.shape[0])


def block_at(flip, sibling):
    chip, core = lax.div(lax.axis_index("tgt"), 2), lax.rem(lax.axis_index("tgt"), 2)
    return 2 * lax.bitwise_xor(chip, flip) + (1 - core if sibling else core)


def weighted(table, q_ref, col_scale, b):
    slots = q_ref.shape[1]
    entries = [table[b * slots + k] for k in range(slots)]
    return [(t, q_ref[b, k] * col_scale[pl.ds(t, 1), :]) for k, t in enumerate(entries)]


def project(table, q_ref, col_scale, tgt, block, outs, width):
    weights = weighted(table, q_ref, col_scale, block)
    rows = [(t, w.astype(jnp.bfloat16)) for t, w in weights]
    total = functools.reduce(jnp.add, [fold_lanes(w, jnp.add) for _, w in weights])
    mass = jnp.broadcast_to(lane_total(total), (SUB, BLK))
    for n, out in enumerate(outs):
        columns = slice(n * width, (n + 1) * width)
        terms = [
            jnp.dot(w, tgt[t, :, columns], preferred_element_type=jnp.float32) for t, w in rows
        ]
        out[:BLK, :] = functools.reduce(jnp.add, terms)
        out[BLK:, :BLK] = mass
        out[BLK:, BLK:] = jnp.zeros((SUB, width - BLK), jnp.float32)


def far_kernel(table, q_ref, col_parts, tgt, col_scale, own, other):
    col_scale[...] = 1.0 / add_parts(col_parts[...])
    for sibling, out in ((True, other), (False, own)):
        halves = [out.at[0], out.at[1]]
        project(table, q_ref, col_scale, tgt, block_at(2, sibling), halves, out.shape[2])


def block_kernel(flip, table, q_ref, col_scale, tgt, own, other):
    for sibling, out in ((True, other), (False, own)):
        project(table, q_ref, col_scale, tgt, block_at(flip, sibling), [out], out.shape[1])


def far_sum_kernel(own, other, low, high):
    low[...] = own[0] + other[0]
    high[...] = own[1] + other[1]


def side_sum_kernel(way, own, other, received, out):
    width = received.shape[1]
    for n in range(2):
        columns = slice(n * width, (n + 1) * width)
        total = own[:, columns] + other[:, columns]
        out[:, columns] = total + received[...] if n == way else total


def finish_kernel(first, second, own, other, out):
    mass = (first[BLK:] + second[BLK:] + own[BLK:] + other[BLK:])[0:1, :BLK]
    total = first[:BLK] + second[:BLK] + own[:BLK] + other[:BLK]
    out[...] = total * to_sublanes(1.0 / mass)


def in_vmem(x):
    return pltpu.with_memory_space_constraint(x, pltpu.VMEM)


def in_hbm(x):
    return pltpu.with_memory_space_constraint(x, pltpu.HBM)


def f32(*shape):
    return jax.ShapeDtypeStruct(shape, jnp.float32)


def v32(*shape):
    return pltpu.VMEM(shape, jnp.float32)


def exchange(copies, axis):
    return in_vmem(lax.all_to_all(copies, axis, 0, 0))


def merge_kernel(merge, own, other, tiles, out, kept):
    merged = merge(jnp.concatenate([own[...], other[...]], axis=0))
    for d in range(out.shape[0]):
        out[d] = merged


def exchange_cols(cols, merge, tiles):
    pairs = [(i, i ^ 3) for i in range(X_HALVES**2)]
    sends, tiles = pl.pallas_call(
        functools.partial(merge_kernel, merge),
        in_specs=[VMEM] * 3,
        out_specs=[VMEM] * 2,
        out_shape=[
            v32(lax.axis_size(GATHER), *cols.shape[1:]),
            pltpu.VMEM(tiles.shape, jnp.float32),
        ],
        input_output_aliases={2: 1},
        compiler_params=PARAMS,
        name="merge",
    )(in_vmem(cols), in_vmem(lax.ppermute(in_vmem(cols), X_AXES, pairs)), tiles)
    return exchange(sends, GATHER), in_vmem(tiles)


def local(sources, targets, block_lists, live_counts):
    src_rows, features = sources.shape
    src_blocks = src_rows // BLK
    tgt_blocks = targets.shape[0] // BLK
    slots = block_lists.shape[2]
    n_src, n_gather, n_tgt = (lax.axis_size(a) for a in (SRC, GATHER, "tgt"))
    total_src = src_rows * n_src
    total_tgt = targets.shape[0] * n_tgt
    src_blocked = sources.reshape(src_blocks, BLK, features)
    tgt_blocked = targets.reshape(tgt_blocks, BLK, features)
    lists = (block_lists[:, 0, :].T, live_counts.T)
    tiles = v32(src_blocks, slots, BLK, BLK)
    row_shape, col_shape = v32(src_blocks, BLK), v32(tgt_blocks, BLK)
    row_sends, col_sends = v32(n_tgt, src_blocks, BLK), v32(1, tgt_blocks, BLK)
    row_scratch, col_scratch = v32(src_blocks, SUB, BLK), v32(tgt_blocks, SUB, BLK)

    tgt_vmem, z, rows, table = pl.pallas_call(
        functools.partial(cost_kernel, features=features),
        in_specs=[HBM] * 4,
        out_specs=[VMEM, VMEM, VMEM, SMEM],
        out_shape=[
            pltpu.VMEM(tgt_blocked.shape, jnp.bfloat16),
            tiles,
            row_sends,
            pltpu.SMEM((src_blocks * slots,), jnp.int32),
        ],
        scratch_shapes=[
            pltpu.SMEM((slots, src_blocks), jnp.int32),
            pltpu.SMEM((1, src_blocks), jnp.int32),
            pltpu.SMEM((src_blocks * slots,), jnp.int32),
            pltpu.SMEM((tgt_blocks,), jnp.int32),
            pltpu.VMEM(src_blocked.shape, jnp.bfloat16),
            col_scratch,
            row_scratch,
            pltpu.SemaphoreType.DMA((tgt_blocks + src_blocks,)),
            pltpu.SemaphoreType.DMA((2,)),
        ],
        compiler_params=PARAMS,
        name="cost",
    )(*[in_hbm(x) for x in (*lists, src_blocked, tgt_blocked)])
    table = pltpu.with_memory_space_constraint(table, pltpu.SMEM)

    w, row_lse, cols = pl.pallas_call(
        first_col_kernel,
        in_specs=[SMEM, VMEM, VMEM],
        out_specs=[VMEM, VMEM, VMEM],
        out_shape=[tiles, f32(src_blocks, BLK), col_sends],
        scratch_shapes=[col_scratch, col_scratch],
        input_output_aliases={1: 0},
        compiler_params=PARAMS,
        name="first_col",
    )(table, in_vmem(z), exchange(rows, "tgt"))

    col_parts, w = exchange_cols(cols, merge_lse, in_vmem(w))
    q, col_lse, rows = pl.pallas_call(
        first_row_kernel,
        in_specs=[SMEM, VMEM, VMEM],
        out_specs=[VMEM, VMEM, VMEM],
        out_shape=[tiles, f32(tgt_blocks, BLK), row_sends],
        scratch_shapes=[row_scratch],
        input_output_aliases={1: 0},
        compiler_params=PARAMS,
        name="first_row",
    )(table, w, col_parts)
    q = in_vmem(q)

    for sweep in range(1, ITERS):
        row_scale, cols = pl.pallas_call(
            functools.partial(col_kernel, share=total_tgt / total_src),
            in_specs=[SMEM, VMEM, VMEM],
            out_specs=[VMEM, VMEM],
            out_shape=[row_shape, col_sends],
            scratch_shapes=[col_scratch],
            compiler_params=PARAMS,
            name="col_sums",
        )(table, q, exchange(rows, "tgt"))
        col_parts, q = exchange_cols(cols, add_parts, q)
        if sweep < ITERS - 1:
            col_scale, rows = pl.pallas_call(
                row_kernel,
                in_specs=[SMEM, VMEM, VMEM],
                out_specs=[VMEM, VMEM],
                out_shape=[col_shape, row_sends],
                scratch_shapes=[row_scratch],
                compiler_params=PARAMS,
                name="row_sums",
            )(table, q, col_parts)

    tgt_vmem = in_vmem(tgt_vmem)
    block = v32(BLK + SUB, features)
    halves = v32(2, BLK + SUB, features // 2)
    half = v32(BLK + SUB, features // 2)

    def swap(x, flip=1):
        return in_vmem(lax.ppermute(x, "tgt", [(t, t ^ flip) for t in range(n_tgt)]))

    def call(kernel, name, operands, out_shape, spec=VMEM):
        return pl.pallas_call(
            kernel,
            in_specs=[spec] + [VMEM] * (len(operands) - 1),
            out_specs=[VMEM] * len(out_shape),
            out_shape=out_shape,
            compiler_params=PARAMS,
            name=name,
        )(*operands)

    col_scale, own_far, other_far = call(
        far_kernel, "far", [table, q, col_parts, tgt_vmem], [col_shape, halves, halves], SMEM
    )
    sides = []
    for flip in (1, 3):
        sides.append(
            call(
                functools.partial(block_kernel, flip),
                "side",
                [table, q, in_vmem(col_scale), tgt_vmem],
                [block, block],
                SMEM,
            )
        )
    low, high = call(
        far_sum_kernel, "far_sum", [in_vmem(own_far), swap(other_far)], [half, half]
    )
    (low, high), sides, col_scale = lax.optimization_barrier(((low, high), sides, col_scale))
    low, high = swap(low, 2), swap(high, 6)
    own_end, other_end = call(
        functools.partial(block_kernel, 0),
        "end",
        [table, q, in_vmem(col_scale), tgt_vmem],
        [block, block],
        SMEM,
    )
    first, second = [
        call(
            functools.partial(side_sum_kernel, way),
            "side_sum",
            [in_vmem(own), swap(other), received],
            [block],
        )[0]
        for way, (own, other), received in ((1, sides[0], high), (0, sides[1], low))
    ]
    mapped = call(
        finish_kernel,
        "finish",
        [swap(first, 2), swap(second, 6), in_vmem(own_end), swap(other_end)],
        [f32(BLK, features)],
    )[0]

    src_square = jnp.sum(jnp.square(sources.astype(jnp.float32)), -1)
    row_potential = (
        EPSILON * (jnp.log(row_scale) - LN2 * row_lse - math.log(total_src))
    ).reshape(src_rows) + src_square / features
    col_potential = EPSILON * (
        jnp.log(col_scale) - LN2 * col_lse + (math.log(total_src) - math.log(total_tgt))
    )
    return (mapped, row_potential, col_potential.reshape(tgt_blocks * BLK))


def solution(mesh):
    n_src, n_tgt = mesh.shape["src"], mesh.shape["tgt"]
    n_z = n_src // X_HALVES**2
    grid = Mesh(mesh.devices.reshape(n_z, X_HALVES, X_HALVES, n_tgt), (*SRC, "tgt"))
    in_specs = (P(SRC, None), P("tgt", None), P(SRC, "tgt", None), P(SRC, "tgt"))
    out_specs = (P((*SRC, "tgt"), None), P(SRC), P("tgt"))
    return jax.shard_map(local, mesh=grid, in_specs=in_specs, out_specs=out_specs, check_vma=False)
```

```python
import functools
import math

import jax
import jax.numpy as jnp
from jax import lax
from jax.experimental import pallas as pl
from jax.experimental.pallas import tpu as pltpu
from jax.sharding import Mesh
from jax.sharding import PartitionSpec as P

BLK = 256
ITERS = 3
EPSILON = 0.1
NEGATIVE = -1e30
LOG2E = math.log2(math.e)
LN2 = math.log(2.0)
LANES = 128
SUB = 8
GROUP = 8
X_HALVES = 2
X_AXES = ("x_high", "x_low")
SRC = ("z", *X_AXES)
GATHER = ("z", "x_low")

VMEM = pl.BlockSpec(memory_space=pltpu.VMEM)
SMEM = pl.BlockSpec(memory_space=pltpu.SMEM)
HBM = pl.BlockSpec(memory_space=pltpu.HBM)
PARAMS = pltpu.CompilerParams(vmem_limit_bytes=12 * 1024 * 1024)
NT_DIMS = (((1,), (1,)), ((), ()))


def eye():
    shape = (LANES, LANES)
    return lax.broadcasted_iota(jnp.int32, shape, 0) == lax.broadcasted_iota(jnp.int32, shape, 1)


def lane_halves(x):
    return [x[:, h : h + LANES] for h in range(0, x.shape[1], LANES)]


def to_lanes(column):
    mask = eye()
    halves = [
        jnp.sum(jnp.where(mask, column[h : h + LANES], 0.0), axis=0, keepdims=True)
        for h in range(0, BLK, LANES)
    ]
    return jnp.concatenate(halves, axis=1)


def to_sublanes(row):
    mask = eye()
    halves = [
        jnp.sum(jnp.where(mask, half, 0.0), axis=1, keepdims=True) for half in lane_halves(row)
    ]
    return jnp.concatenate(halves, axis=0)


def along_rows(row):
    halves = [
        jnp.transpose(jnp.broadcast_to(half, (LANES, LANES))) for half in lane_halves(row)
    ]
    column = jnp.concatenate(halves, axis=0)
    return jnp.concatenate([column] * (BLK // LANES), axis=1)


def lane_total(x):
    halves = [
        jnp.sum(jnp.transpose(x[h : h + LANES]), axis=0, keepdims=True)
        for h in range(0, BLK, LANES)
    ]
    return jnp.concatenate(halves, axis=1)


def fold_rows(tile, op):
    parts = [tile[r : r + SUB] for r in range(0, BLK, SUB)]
    while len(parts) > 1:
        parts = [op(parts[i], parts[i + 1]) for i in range(0, len(parts), 2)]
    return parts[0]


def fold_lanes(tile, op):
    return functools.reduce(op, lane_halves(tile))


def add_parts(values):
    pairs = [values[i] + values[i + 1] for i in range(0, values.shape[0], 2)]
    return functools.reduce(jnp.add, pairs)


def merge_lse(values):
    peak = jnp.max(values, axis=0)
    return peak + jnp.log2(add_parts(jnp.exp2(values - peak[None])))


def spread(out, scratch, n):
    packed = jnp.concatenate([scratch[i, 0:1, :] for i in range(scratch.shape[0])], axis=0)
    for d in range(n):
        out[d] = packed


def cost_kernel(
    lists_hbm, counts_hbm, src_hbm, tgt_hbm,
    tgt, z_ref, rows, table,
    lists, counts, order, place, src, bias, totals, sems, list_sems,
    *, features,
):
    tgt_blocks, src_blocks, slots = tgt.shape[0], src.shape[0], z_ref.shape[1]
    share = tgt_blocks * GROUP // (src_blocks * slots)
    list_copies = [
        pltpu.make_async_copy(lists_hbm, lists, list_sems.at[0]),
        pltpu.make_async_copy(counts_hbm, counts, list_sems.at[1]),
    ]

    def tgt_copy(t):
        return pltpu.make_async_copy(tgt_hbm.at[t], tgt.at[t], sems.at[t])

    def src_copy(b):
        return pltpu.make_async_copy(src_hbm.at[b], src.at[b], sems.at[tgt_blocks + b])

    for copy in list_copies:
        copy.start()
    for b in range(src_blocks):
        src_copy(b).start()
    for t in range(tgt_blocks):
        tgt_copy(t).start()
    for copy in list_copies:
        copy.wait()

    for t in range(tgt_blocks):
        place[t] = 0
    for b in range(src_blocks):
        for k in range(slots):
            t = jnp.where(k < counts[0, b], lists[k, b], lists[0, b])
            table[b * slots + k] = t
            place[t] = place[t] + 1
    start = 0
    for t in range(tgt_blocks):
        count = place[t]
        place[t] = start
        start = start + count
    for n in range(src_blocks * slots):
        t = table[n]
        order[place[t]] = n
        place[t] = place[t] + 1

    for b in range(src_blocks):
        src_copy(b).wait()
    scale = LOG2E / (features * EPSILON)

    def arrived(t, carry):
        tgt_copy(t).wait()
        return carry

    def cross_terms(g, ready):
        entries = [order[g * GROUP + i] for i in range(GROUP)]
        blocks = [table[n] for n in entries]
        squares = [g * share + i for i in range(share)]
        needed = jnp.maximum(ready, jnp.maximum(squares[-1], blocks[-1]) + 1)
        lax.fori_loop(ready, needed, arrived, 0)
        for n, block in zip(entries, blocks):
            z_ref[n // slots, n % slots] = lax.dot_general(
                src[n // slots], tgt[block], NT_DIMS, preferred_element_type=jnp.float32
            )
        for t in squares:
            y = tgt[t].astype(jnp.float32)
            square = fold_lanes(y * y, jnp.add)
            bias[t] = jnp.broadcast_to(-scale * lane_total(square), (SUB, BLK))
        return needed

    lax.fori_loop(0, src_blocks * slots // GROUP, cross_terms, 0)

    @pl.loop(0, src_blocks, unroll=4)
    def _(b):
        peak = None
        for k in range(slots):
            live = k < counts[0, b]
            offset = jnp.where(live, bias[table[b * slots + k], 0:1, :], NEGATIVE)
            z = (2.0 * scale) * z_ref[b, k] + offset
            z_ref[b, k] = z
            top = fold_lanes(z, jnp.maximum)
            peak = top if peak is None else jnp.maximum(peak, top)
        peak = jnp.max(peak, axis=1, keepdims=True)
        total = None
        for k in range(slots):
            part = fold_lanes(jnp.exp2(z_ref[b, k] - peak), jnp.add)
            total = part if total is None else total + part
        lse = to_lanes(peak) + jnp.log2(lane_total(total))
        totals[b] = jnp.broadcast_to(lse, (SUB, BLK))

    spread(rows, totals, rows.shape[0])


def first_col_kernel(table, z_ref, row_parts, w_ref, cols, peaks, sums):
    src_blocks, slots, tgt_blocks = row_parts.shape[1], z_ref.shape[1], peaks.shape[0]
    row_lse = w_ref.at[src_blocks, 0]
    row_lse[:src_blocks, :] = merge_lse(row_parts[...])
    peaks[...] = jnp.full(peaks.shape, NEGATIVE, jnp.float32)
    sums[...] = jnp.zeros(sums.shape, jnp.float32)

    @pl.loop(0, src_blocks)
    def _(b):
        shift = along_rows(row_lse[pl.ds(b, 1), :])
        for k in range(slots):
            t = table[b * slots + k]
            w = z_ref[b, k] - shift
            w_ref[b, k] = w
            top = jnp.max(fold_rows(w, jnp.maximum), axis=0, keepdims=True)
            total = fold_rows(jnp.exp2(w - top), jnp.add)
            old = peaks[t]
            new = jnp.maximum(old, top)
            peaks[t] = new
            sums[t] = sums[t] * jnp.exp2(old - new) + total * jnp.exp2(top - new)

    for t in range(tgt_blocks):
        total = jnp.sum(sums[t], axis=0, keepdims=True)
        lse = jnp.where(total > 0.0, peaks[t, 0:1, :] + jnp.log2(total), NEGATIVE)
        sums[t] = jnp.broadcast_to(lse, (SUB, BLK))
    spread(cols, sums, cols.shape[0])


def row_totals(table, tile, totals, src_blocks, slots):
    @pl.loop(0, src_blocks)
    def _(b):
        total = None
        for k in range(slots):
            t = table[b * slots + k]
            part = fold_lanes(tile(b, k, t), jnp.add)
            total = part if total is None else total + part
        totals[b] = jnp.broadcast_to(lane_total(total), (SUB, BLK))


def first_row_kernel(table, w_ref, col_parts, q_ref, rows, totals):
    src_blocks = totals.shape[0]
    col_lse = q_ref.at[src_blocks, 1]
    col_lse[: col_parts.shape[1], :] = merge_lse(col_parts[...])

    def tile(b, k, t):
        q = jnp.exp2(w_ref[b, k] - col_lse[pl.ds(t, 1), :])
        q_ref[b, k] = q
        return q

    row_totals(table, tile, totals, src_blocks, w_ref.shape[1])
    spread(rows, totals, rows.shape[0])


def col_kernel(table, q_ref, row_parts, row_scale, cols, sums, *, share):
    src_blocks, slots, tgt_blocks = row_scale.shape[0], q_ref.shape[1], sums.shape[0]
    row_scale[...] = share / add_parts(row_parts[...])
    sums[...] = jnp.zeros(sums.shape, jnp.float32)

    @pl.loop(0, src_blocks)
    def _(b):
        scale = along_rows(row_scale[pl.ds(b, 1), :])
        for k in range(slots):
            t = table[b * slots + k]
            sums[t] += fold_rows(q_ref[b, k] * scale, jnp.add)

    for t in range(tgt_blocks):
        sums[t] = jnp.broadcast_to(jnp.sum(sums[t], axis=0, keepdims=True), (SUB, BLK))
    spread(cols, sums, cols.shape[0])


def inner_col_kernel(table, q_ref, row_parts, cols, sums, row_scale, *, share):
    col_kernel(table, q_ref, row_parts, row_scale, cols, sums, share=share)


def row_kernel(table, q_ref, col_parts, rows, totals, col_scale):
    col_scale[...] = 1.0 / add_parts(col_parts[...])

    def tile(b, k, t):
        return q_ref[b, k] * col_scale[pl.ds(t, 1), :]

    row_totals(table, tile, totals, totals.shape[0], q_ref.shape[1])
    spread(rows, totals, rows.shape[0])


def block_at(flip, sibling):
    chip, core = lax.div(lax.axis_index("tgt"), 2), lax.rem(lax.axis_index("tgt"), 2)
    return 2 * lax.bitwise_xor(chip, flip) + (1 - core if sibling else core)


def weighted(table, q_ref, col_scale, b):
    slots = q_ref.shape[1]
    entries = [table[b * slots + k] for k in range(slots)]
    return [(t, q_ref[b, k] * col_scale[pl.ds(t, 1), :]) for k, t in enumerate(entries)]


def project(table, q_ref, col_scale, tgt, block, outs, width):
    weights = weighted(table, q_ref, col_scale, block)
    rows = [(t, w.astype(jnp.bfloat16)) for t, w in weights]
    total = functools.reduce(jnp.add, [fold_lanes(w, jnp.add) for _, w in weights])
    mass = jnp.broadcast_to(lane_total(total), (SUB, BLK))
    terms = [jnp.dot(w, tgt[t], preferred_element_type=jnp.float32) for t, w in rows]
    result = functools.reduce(jnp.add, terms)
    for n, out in enumerate(outs):
        out[:BLK, :] = result[:, n * width : (n + 1) * width]
        out[BLK:, :BLK] = mass
        out[BLK:, BLK:] = jnp.zeros((SUB, width - BLK), jnp.float32)


def far_kernel(table, q_ref, col_parts, tgt, col_scale, own, other):
    col_scale[...] = 1.0 / add_parts(col_parts[...])
    block_kernel(2, table, q_ref, col_scale, tgt, own, other)


def block_kernel(flip, table, q_ref, col_scale, tgt, own, other):
    for sibling, out in ((True, other), (False, own)):
        halves = [out.at[0], out.at[1]]
        project(table, q_ref, col_scale, tgt, block_at(flip, sibling), halves, out.shape[2])


def end_kernel(table, q_ref, col_scale, tgt, own, other, row_lse, col_lse):
    block_kernel(0, table, q_ref, col_scale, tgt, own, other)
    aux = q_ref.at[row_lse.shape[0]]
    row_lse[...] = aux[0, : row_lse.shape[0], :]
    col_lse[...] = aux[1, : col_lse.shape[0], :]


def far_sum_kernel(own, other, low, high):
    low[...] = own[0] + other[0]
    high[...] = own[1] + other[1]


def near_sum_kernel(own_first, other_first, own_second, other_second, low, high):
    low[...] = own_first[0] + other_first[0]
    high[...] = own_second[1] + other_second[1]


def relay_sum_kernel(way, own, other, received, out):
    out[...] = own[way] + other[way] + received[...]


def near_kernel(low, high, out):
    out[0] = low[...]
    out[1] = high[...]


def finish_kernel(near, own, other, relay_low, relay_high, out_hbm, out, sems):
    mass = near[0, BLK:] + own[0, BLK:] + other[0, BLK:] + relay_low[BLK:]
    scale = to_sublanes(1.0 / mass[0:1, :BLK])
    width = relay_low.shape[1]
    rows = BLK // sems.shape[0]
    copies = []
    for n in range(sems.shape[0]):
        part = pl.ds(n * rows, rows)
        for way, relay in enumerate((relay_low, relay_high)):
            total = near[way, part] + own[way, part] + other[way, part] + relay[part]
            out[part, way * width : (way + 1) * width] = total * scale[n * rows : (n + 1) * rows]
        copies.append(pltpu.make_async_copy(out.at[part], out_hbm.at[part], sems.at[n]))
        copies[-1].start()
    for copy in copies:
        copy.wait()


def in_vmem(x):
    return pltpu.with_memory_space_constraint(x, pltpu.VMEM)


def in_hbm(x):
    return pltpu.with_memory_space_constraint(x, pltpu.HBM)


def f32(*shape):
    return jax.ShapeDtypeStruct(shape, jnp.float32)


def v32(*shape):
    return pltpu.VMEM(shape, jnp.float32)


def exchange(copies, axis):
    return in_vmem(lax.all_to_all(copies, axis, 0, 0))


def merge_kernel(merge, own, other, tiles, out, kept):
    merged = merge(jnp.concatenate([own[...], other[...]], axis=0))
    for d in range(out.shape[0]):
        out[d] = merged


def exchange_cols(cols, merge, tiles):
    pairs = [(i, i ^ 3) for i in range(X_HALVES**2)]
    sends, tiles = pl.pallas_call(
        functools.partial(merge_kernel, merge),
        in_specs=[VMEM] * 3,
        out_specs=[VMEM] * 2,
        out_shape=[
            v32(lax.axis_size(GATHER), *cols.shape[1:]),
            pltpu.VMEM(tiles.shape, jnp.float32),
        ],
        input_output_aliases={2: 1},
        compiler_params=PARAMS,
        name="merge",
    )(in_vmem(cols), in_vmem(lax.ppermute(in_vmem(cols), X_AXES, pairs)), tiles)
    return exchange(sends, GATHER), in_vmem(tiles)


def local(sources, targets, block_lists, live_counts):
    src_rows, features = sources.shape
    src_blocks = src_rows // BLK
    tgt_blocks = targets.shape[0] // BLK
    slots = block_lists.shape[2]
    n_src, n_gather, n_tgt = (lax.axis_size(a) for a in (SRC, GATHER, "tgt"))
    total_src = src_rows * n_src
    total_tgt = targets.shape[0] * n_tgt
    src_blocked = sources.reshape(src_blocks, BLK, features)
    tgt_blocked = targets.reshape(tgt_blocks, BLK, features)
    lists = (block_lists[:, 0, :].T, live_counts.T)
    tiles = v32(src_blocks + 1, slots, BLK, BLK)
    row_shape, col_shape = v32(src_blocks, BLK), v32(tgt_blocks, BLK)
    row_sends, col_sends = v32(n_tgt, src_blocks, BLK), v32(1, tgt_blocks, BLK)
    row_scratch, col_scratch = v32(src_blocks, SUB, BLK), v32(tgt_blocks, SUB, BLK)

    tgt_vmem, z, rows, table = pl.pallas_call(
        functools.partial(cost_kernel, features=features),
        in_specs=[HBM] * 4,
        out_specs=[VMEM, VMEM, VMEM, SMEM],
        out_shape=[
            pltpu.VMEM(tgt_blocked.shape, jnp.bfloat16),
            tiles,
            row_sends,
            pltpu.SMEM((src_blocks * slots,), jnp.int32),
        ],
        scratch_shapes=[
            pltpu.SMEM((slots, src_blocks), jnp.int32),
            pltpu.SMEM((1, src_blocks), jnp.int32),
            pltpu.SMEM((src_blocks * slots,), jnp.int32),
            pltpu.SMEM((tgt_blocks,), jnp.int32),
            pltpu.VMEM(src_blocked.shape, jnp.bfloat16),
            col_scratch,
            row_scratch,
            pltpu.SemaphoreType.DMA((tgt_blocks + src_blocks,)),
            pltpu.SemaphoreType.DMA((2,)),
        ],
        compiler_params=PARAMS,
        name="cost",
    )(*[in_hbm(x) for x in (*lists, src_blocked, tgt_blocked)])
    table = pltpu.with_memory_space_constraint(table, pltpu.SMEM)

    w, cols = pl.pallas_call(
        first_col_kernel,
        in_specs=[SMEM, VMEM, VMEM],
        out_specs=[VMEM, VMEM],
        out_shape=[tiles, col_sends],
        scratch_shapes=[col_scratch, col_scratch],
        input_output_aliases={1: 0},
        compiler_params=PARAMS,
        name="first_col",
    )(table, in_vmem(z), exchange(rows, "tgt"))

    col_parts, w = exchange_cols(cols, merge_lse, in_vmem(w))
    q, rows = pl.pallas_call(
        first_row_kernel,
        in_specs=[SMEM, VMEM, VMEM],
        out_specs=[VMEM, VMEM],
        out_shape=[tiles, row_sends],
        scratch_shapes=[row_scratch],
        input_output_aliases={1: 0},
        compiler_params=PARAMS,
        name="first_row",
    )(table, w, col_parts)
    q = in_vmem(q)

    for sweep in range(1, ITERS):
        last = sweep == ITERS - 1
        *scales, cols = pl.pallas_call(
            functools.partial(
                col_kernel if last else inner_col_kernel, share=total_tgt / total_src
            ),
            in_specs=[SMEM, VMEM, VMEM],
            out_specs=[VMEM] * (1 + last),
            out_shape=[row_shape] * last + [col_sends],
            scratch_shapes=[col_scratch] + [row_shape] * (not last),
            compiler_params=PARAMS,
            name="col_sums",
        )(table, q, exchange(rows, "tgt"))
        col_parts, q = exchange_cols(cols, add_parts, q)
        if not last:
            rows = pl.pallas_call(
                row_kernel,
                in_specs=[SMEM, VMEM, VMEM],
                out_specs=VMEM,
                out_shape=row_sends,
                scratch_shapes=[row_scratch, col_shape],
                compiler_params=PARAMS,
                name="row_sums",
            )(table, q, col_parts)
    (row_scale,) = scales

    tgt_vmem = in_vmem(tgt_vmem)
    halves = v32(2, BLK + SUB, features // 2)
    half = v32(BLK + SUB, features // 2)

    def send(x, flip):
        return lax.ppermute(x, "tgt", [(t, t ^ flip) for t in range(n_tgt)])

    def swap(x, flip=1):
        return in_vmem(send(x, flip))

    def call(kernel, name, operands, out_shape, spec=VMEM, cost=None):
        return pl.pallas_call(
            kernel,
            in_specs=[spec] + [VMEM] * (len(operands) - 1),
            out_specs=[VMEM] * len(out_shape),
            out_shape=out_shape,
            compiler_params=PARAMS,
            cost_estimate=cost,
            name=name,
        )(*operands)

    col_scale, own_far, other_far = call(
        far_kernel, "far", [table, q, col_parts, tgt_vmem], [col_shape, halves, halves], SMEM
    )
    sides = []
    for flip in (1, 3):
        sides.append(
            call(
                functools.partial(block_kernel, flip),
                "side",
                [table, q, in_vmem(col_scale), tgt_vmem],
                [halves, halves],
                SMEM,
            )
        )
    low, high = call(
        far_sum_kernel, "far_sum", [in_vmem(own_far), swap(other_far)], [half, half]
    )
    (low, high), sides, col_scale = lax.optimization_barrier(((low, high), sides, col_scale))
    low, high = swap(low, 2), swap(high, 6)
    own_end, other_end, row_lse, col_lse = call(
        end_kernel,
        "end",
        [table, q, in_vmem(col_scale), tgt_vmem],
        [halves, halves, f32(src_blocks, BLK), f32(tgt_blocks, BLK)],
        SMEM,
    )
    sides = [(own, swap(other)) for own, other in sides]
    (own_first, other_first), (own_second, other_second) = sides
    near_low, near_high = call(
        near_sum_kernel,
        "near_sum",
        [in_vmem(own_first), other_first, in_vmem(own_second), other_second],
        [half, half],
    )
    near = call(
        near_kernel,
        "near",
        [swap(near_low, 2), swap(near_high, 6)],
        [halves],
        cost=pl.CostEstimate(flops=3 * 10**9, bytes_accessed=0, transcendentals=0),
    )[0]

    def relay(way, own, other, received, flip):
        kernel = functools.partial(relay_sum_kernel, way)
        total = call(kernel, "relay_sum", [in_vmem(own), other, received], [half])[0]
        return swap(total, flip)

    relay_high = relay(1, own_first, other_first, high, 2)
    relay_low = relay(0, own_second, other_second, low, 6)
    mapped = pl.pallas_call(
        finish_kernel,
        in_specs=[VMEM] * 5,
        out_specs=HBM,
        out_shape=f32(BLK, features),
        scratch_shapes=[v32(BLK, features), pltpu.SemaphoreType.DMA((4,))],
        compiler_params=PARAMS,
        name="finish",
    )(in_vmem(near), in_vmem(own_end), swap(other_end), relay_low, relay_high)

    late_sources, _ = lax.optimization_barrier((sources, near))
    src_square = jnp.sum(jnp.square(late_sources.astype(jnp.float32)), -1)
    row_potential = (
        EPSILON * (jnp.log(row_scale) - LN2 * row_lse - math.log(total_src))
    ).reshape(src_rows) + src_square / features
    col_potential = EPSILON * (
        jnp.log(col_scale) - LN2 * col_lse + (math.log(total_src) - math.log(total_tgt))
    )
    return (mapped, row_potential, col_potential.reshape(tgt_blocks * BLK))


def solution(mesh):
    n_src, n_tgt = mesh.shape["src"], mesh.shape["tgt"]
    n_z = n_src // X_HALVES**2
    grid = Mesh(mesh.devices.reshape(n_z, X_HALVES, X_HALVES, n_tgt), (*SRC, "tgt"))
    in_specs = (P(SRC, None), P("tgt", None), P(SRC, "tgt", None), P(SRC, "tgt"))
    out_specs = (P((*SRC, "tgt"), None), P(SRC), P("tgt"))
    return jax.shard_map(local, mesh=grid, in_specs=in_specs, out_specs=out_specs, check_vma=False)
```

```python
import functools
import math

import jax
import jax.numpy as jnp
from jax import lax
from jax.experimental import pallas as pl
from jax.experimental.pallas import tpu as pltpu
from jax.sharding import Mesh
from jax.sharding import PartitionSpec as P

BLK = 256
ITERS = 3
EPSILON = 0.1
NEGATIVE = -1e30
LOG2E = math.log2(math.e)
LN2 = math.log(2.0)
LANES = 128
SUB = 8
GROUP = 8
X_HALVES = 2
X_AXES = ("x_high", "x_low")
SRC = ("z", *X_AXES)
GATHER = ("z", "x_low")

VMEM = pl.BlockSpec(memory_space=pltpu.VMEM)
SMEM = pl.BlockSpec(memory_space=pltpu.SMEM)
HBM = pl.BlockSpec(memory_space=pltpu.HBM)
PARAMS = pltpu.CompilerParams(vmem_limit_bytes=12 * 1024 * 1024)
NT_DIMS = (((1,), (1,)), ((), ()))


def eye():
    shape = (LANES, LANES)
    return lax.broadcasted_iota(jnp.int32, shape, 0) == lax.broadcasted_iota(jnp.int32, shape, 1)


def lane_halves(x):
    return [x[:, h : h + LANES] for h in range(0, x.shape[1], LANES)]


def to_lanes(column):
    mask = eye()
    halves = [
        jnp.sum(jnp.where(mask, column[h : h + LANES], 0.0), axis=0, keepdims=True)
        for h in range(0, BLK, LANES)
    ]
    return jnp.concatenate(halves, axis=1)


def to_sublanes(row):
    mask = eye()
    halves = [
        jnp.sum(jnp.where(mask, half, 0.0), axis=1, keepdims=True) for half in lane_halves(row)
    ]
    return jnp.concatenate(halves, axis=0)


def along_rows(row):
    halves = [
        jnp.transpose(jnp.broadcast_to(half, (LANES, LANES))) for half in lane_halves(row)
    ]
    column = jnp.concatenate(halves, axis=0)
    return jnp.concatenate([column] * (BLK // LANES), axis=1)


def lane_total(x):
    halves = [
        jnp.sum(jnp.transpose(x[h : h + LANES]), axis=0, keepdims=True)
        for h in range(0, BLK, LANES)
    ]
    return jnp.concatenate(halves, axis=1)


def fold_rows(tile, op):
    parts = [tile[r : r + SUB] for r in range(0, BLK, SUB)]
    while len(parts) > 1:
        parts = [op(parts[i], parts[i + 1]) for i in range(0, len(parts), 2)]
    return parts[0]


def fold_lanes(tile, op):
    return functools.reduce(op, lane_halves(tile))


def add_parts(values):
    pairs = [values[i] + values[i + 1] for i in range(0, values.shape[0], 2)]
    return functools.reduce(jnp.add, pairs)


def merge_lse(values):
    peak = jnp.max(values, axis=0)
    return peak + jnp.log2(add_parts(jnp.exp2(values - peak[None])))


def spread(out, scratch, n):
    packed = jnp.concatenate([scratch[i, 0:1, :] for i in range(scratch.shape[0])], axis=0)
    for d in range(n):
        out[d] = packed


def cost_kernel(
    lists_hbm, counts_hbm, src_hbm, tgt_hbm,
    tgt, z_ref, rows, table,
    lists, counts, order, place, src, bias, totals, sems, list_sems,
    *, features,
):
    tgt_blocks, src_blocks, slots = tgt.shape[0], src.shape[0], z_ref.shape[1]
    share = tgt_blocks * GROUP // (src_blocks * slots)
    list_copies = [
        pltpu.make_async_copy(lists_hbm, lists, list_sems.at[0]),
        pltpu.make_async_copy(counts_hbm, counts, list_sems.at[1]),
    ]

    def tgt_copy(t):
        return pltpu.make_async_copy(tgt_hbm.at[t], tgt.at[t], sems.at[t])

    def src_copy(b):
        return pltpu.make_async_copy(src_hbm.at[b], src.at[b], sems.at[tgt_blocks + b])

    for copy in list_copies:
        copy.start()
    for b in range(src_blocks):
        src_copy(b).start()
    for t in range(tgt_blocks):
        tgt_copy(t).start()
    for copy in list_copies:
        copy.wait()

    for t in range(tgt_blocks):
        place[t] = 0
    for b in range(src_blocks):
        for k in range(slots):
            t = jnp.where(k < counts[0, b], lists[k, b], lists[0, b])
            table[b * slots + k] = t
            place[t] = place[t] + 1
    start = 0
    for t in range(tgt_blocks):
        count = place[t]
        place[t] = start
        start = start + count
    for n in range(src_blocks * slots):
        t = table[n]
        order[place[t]] = n
        place[t] = place[t] + 1

    for b in range(src_blocks):
        src_copy(b).wait()
    scale = LOG2E / (features * EPSILON)

    def arrived(t, carry):
        tgt_copy(t).wait()
        return carry

    def cross_terms(g, ready):
        entries = [order[g * GROUP + i] for i in range(GROUP)]
        blocks = [table[n] for n in entries]
        squares = [g * share + i for i in range(share)]
        needed = jnp.maximum(ready, jnp.maximum(squares[-1], blocks[-1]) + 1)
        lax.fori_loop(ready, needed, arrived, 0)
        for n, block in zip(entries, blocks):
            z_ref[n // slots, n % slots] = lax.dot_general(
                src[n // slots], tgt[block], NT_DIMS, preferred_element_type=jnp.float32
            )
        for t in squares:
            y = tgt[t].astype(jnp.float32)
            square = fold_lanes(y * y, jnp.add)
            bias[t] = jnp.broadcast_to(-scale * lane_total(square), (SUB, BLK))
        return needed

    lax.fori_loop(0, src_blocks * slots // GROUP, cross_terms, 0)

    @pl.loop(0, src_blocks, unroll=4)
    def _(b):
        peak = None
        for k in range(slots):
            live = k < counts[0, b]
            offset = jnp.where(live, bias[table[b * slots + k], 0:1, :], NEGATIVE)
            z = (2.0 * scale) * z_ref[b, k] + offset
            z_ref[b, k] = z
            top = fold_lanes(z, jnp.maximum)
            peak = top if peak is None else jnp.maximum(peak, top)
        peak = jnp.max(peak, axis=1, keepdims=True)
        total = None
        for k in range(slots):
            part = fold_lanes(jnp.exp2(z_ref[b, k] - peak), jnp.add)
            total = part if total is None else total + part
        lse = to_lanes(peak) + jnp.log2(lane_total(total))
        totals[b] = jnp.broadcast_to(lse, (SUB, BLK))

    spread(rows, totals, rows.shape[0])


def first_col_kernel(table, z_ref, row_parts, w_ref, cols, peaks, sums):
    src_blocks, slots, tgt_blocks = row_parts.shape[1], z_ref.shape[1], peaks.shape[0]
    row_lse = w_ref.at[src_blocks, 0]
    row_lse[:src_blocks, :] = merge_lse(row_parts[...])
    peaks[...] = jnp.full(peaks.shape, NEGATIVE, jnp.float32)
    sums[...] = jnp.zeros(sums.shape, jnp.float32)

    @pl.loop(0, src_blocks)
    def _(b):
        shift = along_rows(row_lse[pl.ds(b, 1), :])
        for k in range(slots):
            t = table[b * slots + k]
            w = z_ref[b, k] - shift
            w_ref[b, k] = w
            top = jnp.max(fold_rows(w, jnp.maximum), axis=0, keepdims=True)
            total = fold_rows(jnp.exp2(w - top), jnp.add)
            old = peaks[t]
            new = jnp.maximum(old, top)
            peaks[t] = new
            sums[t] = sums[t] * jnp.exp2(old - new) + total * jnp.exp2(top - new)

    for t in range(tgt_blocks):
        total = jnp.sum(sums[t], axis=0, keepdims=True)
        lse = jnp.where(total > 0.0, peaks[t, 0:1, :] + jnp.log2(total), NEGATIVE)
        sums[t] = jnp.broadcast_to(lse, (SUB, BLK))
    spread(cols, sums, cols.shape[0])


def row_totals(table, tile, totals, src_blocks, slots):
    @pl.loop(0, src_blocks)
    def _(b):
        total = None
        for k in range(slots):
            t = table[b * slots + k]
            part = fold_lanes(tile(b, k, t), jnp.add)
            total = part if total is None else total + part
        totals[b] = jnp.broadcast_to(lane_total(total), (SUB, BLK))


def first_row_kernel(table, w_ref, col_parts, q_ref, rows, totals):
    src_blocks = totals.shape[0]
    col_lse = q_ref.at[src_blocks, 1]
    col_lse[: col_parts.shape[1], :] = merge_lse(col_parts[...])

    def tile(b, k, t):
        q = jnp.exp2(w_ref[b, k] - col_lse[pl.ds(t, 1), :])
        q_ref[b, k] = q
        return q

    row_totals(table, tile, totals, src_blocks, w_ref.shape[1])
    spread(rows, totals, rows.shape[0])


def col_kernel(table, q_ref, row_parts, row_scale, cols, sums, *, share):
    src_blocks, slots, tgt_blocks = row_scale.shape[0], q_ref.shape[1], sums.shape[0]
    row_scale[...] = share / add_parts(row_parts[...])
    sums[...] = jnp.zeros(sums.shape, jnp.float32)

    @pl.loop(0, src_blocks)
    def _(b):
        scale = along_rows(row_scale[pl.ds(b, 1), :])
        for k in range(slots):
            t = table[b * slots + k]
            sums[t] += fold_rows(q_ref[b, k] * scale, jnp.add)

    for t in range(tgt_blocks):
        sums[t] = jnp.broadcast_to(jnp.sum(sums[t], axis=0, keepdims=True), (SUB, BLK))
    spread(cols, sums, cols.shape[0])


def inner_col_kernel(table, q_ref, row_parts, cols, sums, row_scale, *, share):
    col_kernel(table, q_ref, row_parts, row_scale, cols, sums, share=share)


def row_kernel(table, q_ref, col_parts, rows, totals, col_scale):
    col_scale[...] = 1.0 / add_parts(col_parts[...])

    def tile(b, k, t):
        return q_ref[b, k] * col_scale[pl.ds(t, 1), :]

    row_totals(table, tile, totals, totals.shape[0], q_ref.shape[1])
    spread(rows, totals, rows.shape[0])


def block_at(flip, sibling):
    chip, core = lax.div(lax.axis_index("tgt"), 2), lax.rem(lax.axis_index("tgt"), 2)
    return 2 * lax.bitwise_xor(chip, flip) + (1 - core if sibling else core)


def weighted(table, q_ref, col_scale, b):
    slots = q_ref.shape[1]
    entries = [table[b * slots + k] for k in range(slots)]
    return [(t, q_ref[b, k] * col_scale[pl.ds(t, 1), :]) for k, t in enumerate(entries)]


def project(table, q_ref, col_scale, tgt, block, outs, width):
    weights = weighted(table, q_ref, col_scale, block)
    rows = [(t, w.astype(jnp.bfloat16)) for t, w in weights]
    total = functools.reduce(jnp.add, [fold_lanes(w, jnp.add) for _, w in weights])
    mass = jnp.broadcast_to(lane_total(total), (SUB, BLK))
    terms = [jnp.dot(w, tgt[t], preferred_element_type=jnp.float32) for t, w in rows]
    result = functools.reduce(jnp.add, terms)
    for n, out in enumerate(outs):
        out[:BLK, :] = result[:, n * width : (n + 1) * width]
        out[BLK:, :BLK] = mass
        out[BLK:, BLK:] = jnp.zeros((SUB, width - BLK), jnp.float32)


def far_kernel(table, q_ref, col_parts, tgt, col_scale, own, other):
    col_scale[...] = 1.0 / add_parts(col_parts[...])
    block_kernel(2, table, q_ref, col_scale, tgt, own, other)


def block_kernel(flip, table, q_ref, col_scale, tgt, own, other):
    for sibling, out in ((True, other), (False, own)):
        halves = [out.at[0], out.at[1]]
        project(table, q_ref, col_scale, tgt, block_at(flip, sibling), halves, out.shape[2])


def end_kernel(table, q_ref, col_scale, tgt, own, other, row_lse, col_lse):
    block_kernel(0, table, q_ref, col_scale, tgt, own, other)
    aux = q_ref.at[row_lse.shape[0]]
    row_lse[...] = aux[0, : row_lse.shape[0], :]
    col_lse[...] = aux[1, : col_lse.shape[0], :]


def far_sum_kernel(own, other, low, high):
    low[...] = own[0] + other[0]
    high[...] = own[1] + other[1]


def near_sum_kernel(own_first, other_first, own_second, other_second, low, high):
    low[...] = own_first[0] + other_first[0]
    high[...] = own_second[1] + other_second[1]


def relay_sum_kernel(way, own, other, received, out):
    out[...] = own[way] + other[way] + received[...]


def near_kernel(low, high, out):
    out[0] = low[...]
    out[1] = high[...]


def finish_kernel(near, own, other, relay_low, relay_high, out_hbm, out, sems):
    mass = near[0, BLK:] + own[0, BLK:] + other[0, BLK:] + relay_low[BLK:]
    scale = to_sublanes(1.0 / mass[0:1, :BLK])
    width = relay_low.shape[1]
    rows = BLK // sems.shape[0]
    copies = []
    for n in range(sems.shape[0]):
        part = pl.ds(n * rows, rows)
        for way, relay in enumerate((relay_low, relay_high)):
            total = near[way, part] + own[way, part] + other[way, part] + relay[part]
            out[part, way * width : (way + 1) * width] = total * scale[n * rows : (n + 1) * rows]
        copies.append(pltpu.make_async_copy(out.at[part], out_hbm.at[part], sems.at[n]))
        copies[-1].start()
    for copy in copies:
        copy.wait()


def in_vmem(x):
    return pltpu.with_memory_space_constraint(x, pltpu.VMEM)


def in_hbm(x):
    return pltpu.with_memory_space_constraint(x, pltpu.HBM)


def f32(*shape):
    return jax.ShapeDtypeStruct(shape, jnp.float32)


def v32(*shape):
    return pltpu.VMEM(shape, jnp.float32)


def exchange(copies, axis):
    return in_vmem(lax.all_to_all(copies, axis, 0, 0))


def merge_kernel(merge, own, other, tiles, out, kept):
    merged = merge(jnp.concatenate([own[...], other[...]], axis=0))
    for d in range(out.shape[0]):
        out[d] = merged


def exchange_cols(cols, merge, tiles):
    pairs = [(i, i ^ 3) for i in range(X_HALVES**2)]
    sends, tiles = pl.pallas_call(
        functools.partial(merge_kernel, merge),
        in_specs=[VMEM] * 3,
        out_specs=[VMEM] * 2,
        out_shape=[
            v32(lax.axis_size(GATHER), *cols.shape[1:]),
            pltpu.VMEM(tiles.shape, jnp.float32),
        ],
        input_output_aliases={2: 1},
        compiler_params=PARAMS,
        name="merge",
    )(in_vmem(cols), in_vmem(lax.ppermute(in_vmem(cols), X_AXES, pairs)), tiles)
    return exchange(sends, GATHER), in_vmem(tiles)


def local(sources, targets, block_lists, live_counts):
    src_rows, features = sources.shape
    src_blocks = src_rows // BLK
    tgt_blocks = targets.shape[0] // BLK
    slots = block_lists.shape[2]
    n_src, n_gather, n_tgt = (lax.axis_size(a) for a in (SRC, GATHER, "tgt"))
    total_src = src_rows * n_src
    total_tgt = targets.shape[0] * n_tgt
    src_blocked = sources.reshape(src_blocks, BLK, features)
    tgt_blocked = targets.reshape(tgt_blocks, BLK, features)
    lists = (block_lists[:, 0, :].T, live_counts.T)
    tiles = v32(src_blocks + 1, slots, BLK, BLK)
    row_shape, col_shape = v32(src_blocks, BLK), v32(tgt_blocks, BLK)
    row_sends, col_sends = v32(n_tgt, src_blocks, BLK), v32(1, tgt_blocks, BLK)
    row_scratch, col_scratch = v32(src_blocks, SUB, BLK), v32(tgt_blocks, SUB, BLK)

    tgt_vmem, z, rows, table = pl.pallas_call(
        functools.partial(cost_kernel, features=features),
        in_specs=[HBM] * 4,
        out_specs=[VMEM, VMEM, VMEM, SMEM],
        out_shape=[
            pltpu.VMEM(tgt_blocked.shape, jnp.bfloat16),
            tiles,
            row_sends,
            pltpu.SMEM((src_blocks * slots,), jnp.int32),
        ],
        scratch_shapes=[
            pltpu.SMEM((slots, src_blocks), jnp.int32),
            pltpu.SMEM((1, src_blocks), jnp.int32),
            pltpu.SMEM((src_blocks * slots,), jnp.int32),
            pltpu.SMEM((tgt_blocks,), jnp.int32),
            pltpu.VMEM(src_blocked.shape, jnp.bfloat16),
            col_scratch,
            row_scratch,
            pltpu.SemaphoreType.DMA((tgt_blocks + src_blocks,)),
            pltpu.SemaphoreType.DMA((2,)),
        ],
        compiler_params=PARAMS,
        name="cost",
    )(*[in_hbm(x) for x in (*lists, src_blocked, tgt_blocked)])
    table = pltpu.with_memory_space_constraint(table, pltpu.SMEM)

    w, cols = pl.pallas_call(
        first_col_kernel,
        in_specs=[SMEM, VMEM, VMEM],
        out_specs=[VMEM, VMEM],
        out_shape=[tiles, col_sends],
        scratch_shapes=[col_scratch, col_scratch],
        input_output_aliases={1: 0},
        compiler_params=PARAMS,
        name="first_col",
    )(table, in_vmem(z), exchange(rows, "tgt"))

    col_parts, w = exchange_cols(cols, merge_lse, in_vmem(w))
    q, rows = pl.pallas_call(
        first_row_kernel,
        in_specs=[SMEM, VMEM, VMEM],
        out_specs=[VMEM, VMEM],
        out_shape=[tiles, row_sends],
        scratch_shapes=[row_scratch],
        input_output_aliases={1: 0},
        compiler_params=PARAMS,
        name="first_row",
    )(table, w, col_parts)
    q = in_vmem(q)

    for sweep in range(1, ITERS):
        last = sweep == ITERS - 1
        *scales, cols = pl.pallas_call(
            functools.partial(
                col_kernel if last else inner_col_kernel, share=total_tgt / total_src
            ),
            in_specs=[SMEM, VMEM, VMEM],
            out_specs=[VMEM] * (1 + last),
            out_shape=[row_shape] * last + [col_sends],
            scratch_shapes=[col_scratch] + [row_shape] * (not last),
            compiler_params=PARAMS,
            name="col_sums",
        )(table, q, exchange(rows, "tgt"))
        col_parts, q = exchange_cols(cols, add_parts, q)
        if not last:
            rows = pl.pallas_call(
                row_kernel,
                in_specs=[SMEM, VMEM, VMEM],
                out_specs=VMEM,
                out_shape=row_sends,
                scratch_shapes=[row_scratch, col_shape],
                compiler_params=PARAMS,
                name="row_sums",
            )(table, q, col_parts)
    (row_scale,) = scales

    tgt_vmem = in_vmem(tgt_vmem)
    halves = v32(2, BLK + SUB, features // 2)
    half = v32(BLK + SUB, features // 2)

    def send(x, flip):
        return lax.ppermute(x, "tgt", [(t, t ^ flip) for t in range(n_tgt)])

    def swap(x, flip=1):
        return in_vmem(send(x, flip))

    def call(kernel, name, operands, out_shape, spec=VMEM, cost=None):
        return pl.pallas_call(
            kernel,
            in_specs=[spec] + [VMEM] * (len(operands) - 1),
            out_specs=[VMEM] * len(out_shape),
            out_shape=out_shape,
            compiler_params=PARAMS,
            cost_estimate=cost,
            name=name,
        )(*operands)

    col_scale, own_far, other_far = call(
        far_kernel, "far", [table, q, col_parts, tgt_vmem], [col_shape, halves, halves], SMEM
    )
    sides = []
    for flip in (1, 3):
        sides.append(
            call(
                functools.partial(block_kernel, flip),
                "side",
                [table, q, in_vmem(col_scale), tgt_vmem],
                [halves, halves],
                SMEM,
            )
        )
    low, high = call(
        far_sum_kernel, "far_sum", [in_vmem(own_far), swap(other_far)], [half, half]
    )
    (low, high), sides, col_scale = lax.optimization_barrier(((low, high), sides, col_scale))
    low, high = swap(low, 2), swap(high, 6)
    own_end, other_end, row_lse, col_lse = call(
        end_kernel,
        "end",
        [table, q, in_vmem(col_scale), tgt_vmem],
        [halves, halves, f32(src_blocks, BLK), f32(tgt_blocks, BLK)],
        SMEM,
    )
    sides = [(own, swap(other)) for own, other in sides]
    (own_first, other_first), (own_second, other_second) = sides
    near_low, near_high = call(
        near_sum_kernel,
        "near_sum",
        [in_vmem(own_first), other_first, in_vmem(own_second), other_second],
        [half, half],
    )
    near = call(
        near_kernel,
        "near",
        [swap(near_low, 2), swap(near_high, 6)],
        [halves],
        cost=pl.CostEstimate(flops=3 * 10**9, bytes_accessed=0, transcendentals=0),
    )[0]

    def relay(way, own, other, received, flip):
        kernel = functools.partial(relay_sum_kernel, way)
        total = call(kernel, "relay_sum", [in_vmem(own), other, received], [half])[0]
        return swap(total, flip)

    relay_high = relay(1, own_first, other_first, high, 2)
    relay_low = relay(0, own_second, other_second, low, 6)
    mapped = pl.pallas_call(
        finish_kernel,
        in_specs=[VMEM] * 5,
        out_specs=HBM,
        out_shape=f32(BLK, features),
        scratch_shapes=[v32(BLK, features), pltpu.SemaphoreType.DMA((4,))],
        compiler_params=PARAMS,
        name="finish",
    )(in_vmem(near), in_vmem(own_end), swap(other_end), relay_low, relay_high)

    late = (sources, row_lse, col_lse, near)
    late_sources, row_lse, col_lse, _ = lax.optimization_barrier(late)
    src_square = jnp.sum(jnp.square(late_sources.astype(jnp.float32)), -1)
    row_potential = (
        EPSILON * (jnp.log(row_scale) - LN2 * row_lse - math.log(total_src))
    ).reshape(src_rows) + src_square / features
    col_potential = EPSILON * (
        jnp.log(col_scale) - LN2 * col_lse + (math.log(total_src) - math.log(total_tgt))
    )
    return (mapped, row_potential, col_potential.reshape(tgt_blocks * BLK))


def solution(mesh):
    n_src, n_tgt = mesh.shape["src"], mesh.shape["tgt"]
    n_z = n_src // X_HALVES**2
    grid = Mesh(mesh.devices.reshape(n_z, X_HALVES, X_HALVES, n_tgt), (*SRC, "tgt"))
    in_specs = (P(SRC, None), P("tgt", None), P(SRC, "tgt", None), P(SRC, "tgt"))
    out_specs = (P((*SRC, "tgt"), None), P(SRC), P("tgt"))
    return jax.shard_map(local, mesh=grid, in_specs=in_specs, out_specs=out_specs, check_vma=False)
```

```python
import functools
import math

import jax
import jax.numpy as jnp
from jax import lax
from jax.experimental import pallas as pl
from jax.experimental.pallas import tpu as pltpu
from jax.sharding import Mesh
from jax.sharding import PartitionSpec as P

BLK = 256
ITERS = 3
EPSILON = 0.1
NEGATIVE = -1e30
LOG2E = math.log2(math.e)
LN2 = math.log(2.0)
LANES = 128
SUB = 8
GROUP = 8
X_HALVES = 2
X_AXES = ("x_high", "x_low")
SRC = ("z", *X_AXES)
GATHER = ("z", "x_low")

VMEM = pl.BlockSpec(memory_space=pltpu.VMEM)
SMEM = pl.BlockSpec(memory_space=pltpu.SMEM)
HBM = pl.BlockSpec(memory_space=pltpu.HBM)
PARAMS = pltpu.CompilerParams(vmem_limit_bytes=12 * 1024 * 1024)
NT_DIMS = (((1,), (1,)), ((), ()))


def eye():
    shape = (LANES, LANES)
    return lax.broadcasted_iota(jnp.int32, shape, 0) == lax.broadcasted_iota(jnp.int32, shape, 1)


def lane_halves(x):
    return [x[:, h : h + LANES] for h in range(0, x.shape[1], LANES)]


def to_lanes(column):
    mask = eye()
    halves = [
        jnp.sum(jnp.where(mask, column[h : h + LANES], 0.0), axis=0, keepdims=True)
        for h in range(0, BLK, LANES)
    ]
    return jnp.concatenate(halves, axis=1)


def to_sublanes(row):
    mask = eye()
    halves = [
        jnp.sum(jnp.where(mask, half, 0.0), axis=1, keepdims=True) for half in lane_halves(row)
    ]
    return jnp.concatenate(halves, axis=0)


def along_rows(row):
    halves = [
        jnp.transpose(jnp.broadcast_to(half, (LANES, LANES))) for half in lane_halves(row)
    ]
    column = jnp.concatenate(halves, axis=0)
    return jnp.concatenate([column] * (BLK // LANES), axis=1)


def lane_total(x):
    halves = [
        jnp.sum(jnp.transpose(x[h : h + LANES]), axis=0, keepdims=True)
        for h in range(0, BLK, LANES)
    ]
    return jnp.concatenate(halves, axis=1)


def fold_rows(tile, op):
    parts = [tile[r : r + SUB] for r in range(0, BLK, SUB)]
    while len(parts) > 1:
        parts = [op(parts[i], parts[i + 1]) for i in range(0, len(parts), 2)]
    return parts[0]


def fold_lanes(tile, op):
    return functools.reduce(op, lane_halves(tile))


def add_parts(values):
    pairs = [values[i] + values[i + 1] for i in range(0, values.shape[0], 2)]
    return functools.reduce(jnp.add, pairs)


def merge_lse(values):
    peak = jnp.max(values, axis=0)
    return peak + jnp.log2(add_parts(jnp.exp2(values - peak[None])))


def spread(out, scratch, n):
    packed = jnp.concatenate([scratch[i, 0:1, :] for i in range(scratch.shape[0])], axis=0)
    for d in range(n):
        out[d] = packed


def cost_kernel(
    lists_hbm, counts_hbm, src_hbm, tgt_hbm,
    tgt, z_ref, rows, table,
    lists, counts, order, place, src, bias, totals, sems, list_sems,
    *, features,
):
    tgt_blocks, src_blocks, slots = tgt.shape[0], src.shape[0], z_ref.shape[1]
    share = tgt_blocks * GROUP // (src_blocks * slots)
    list_copies = [
        pltpu.make_async_copy(lists_hbm, lists, list_sems.at[0]),
        pltpu.make_async_copy(counts_hbm, counts, list_sems.at[1]),
    ]

    def tgt_copy(t):
        return pltpu.make_async_copy(tgt_hbm.at[t], tgt.at[t], sems.at[t])

    def src_copy(b):
        return pltpu.make_async_copy(src_hbm.at[b], src.at[b], sems.at[tgt_blocks + b])

    for copy in list_copies:
        copy.start()
    for b in range(src_blocks):
        src_copy(b).start()
    for t in range(tgt_blocks):
        tgt_copy(t).start()
    for copy in list_copies:
        copy.wait()

    for t in range(tgt_blocks):
        place[t] = 0
    for b in range(src_blocks):
        for k in range(slots):
            t = jnp.where(k < counts[0, b], lists[k, b], lists[0, b])
            table[b * slots + k] = t
            place[t] = place[t] + 1
    start = 0
    for t in range(tgt_blocks):
        count = place[t]
        place[t] = start
        start = start + count
    for n in range(src_blocks * slots):
        t = table[n]
        order[place[t]] = n
        place[t] = place[t] + 1

    for b in range(src_blocks):
        src_copy(b).wait()
    scale = LOG2E / (features * EPSILON)

    def arrived(t, carry):
        tgt_copy(t).wait()
        return carry

    def cross_terms(g, ready):
        entries = [order[g * GROUP + i] for i in range(GROUP)]
        blocks = [table[n] for n in entries]
        squares = [g * share + i for i in range(share)]
        needed = jnp.maximum(ready, jnp.maximum(squares[-1], blocks[-1]) + 1)
        lax.fori_loop(ready, needed, arrived, 0)
        for n, block in zip(entries, blocks):
            z_ref[n // slots, n % slots] = lax.dot_general(
                src[n // slots], tgt[block], NT_DIMS, preferred_element_type=jnp.float32
            )
        for t in squares:
            y = tgt[t].astype(jnp.float32)
            square = fold_lanes(y * y, jnp.add)
            bias[t] = jnp.broadcast_to(-scale * lane_total(square), (SUB, BLK))
        return needed

    lax.fori_loop(0, src_blocks * slots // GROUP, cross_terms, 0)

    @pl.loop(0, src_blocks, unroll=4)
    def _(b):
        peak = None
        for k in range(slots):
            live = k < counts[0, b]
            offset = jnp.where(live, bias[table[b * slots + k], 0:1, :], NEGATIVE)
            z = (2.0 * scale) * z_ref[b, k] + offset
            z_ref[b, k] = z
            top = fold_lanes(z, jnp.maximum)
            peak = top if peak is None else jnp.maximum(peak, top)
        peak = jnp.max(peak, axis=1, keepdims=True)
        total = None
        for k in range(slots):
            part = fold_lanes(jnp.exp2(z_ref[b, k] - peak), jnp.add)
            total = part if total is None else total + part
        lse = to_lanes(peak) + jnp.log2(lane_total(total))
        totals[b] = jnp.broadcast_to(lse, (SUB, BLK))

    spread(rows, totals, rows.shape[0])


def first_col_kernel(table, z_ref, row_parts, w_ref, cols, peaks, sums):
    src_blocks, slots, tgt_blocks = row_parts.shape[1], z_ref.shape[1], peaks.shape[0]
    row_lse = w_ref.at[src_blocks, 0]
    row_lse[:src_blocks, :] = merge_lse(row_parts[...])
    peaks[...] = jnp.full(peaks.shape, NEGATIVE, jnp.float32)
    sums[...] = jnp.zeros(sums.shape, jnp.float32)

    @pl.loop(0, src_blocks, unroll=2)
    def _(b):
        shift = along_rows(row_lse[pl.ds(b, 1), :])
        for k in range(slots):
            t = table[b * slots + k]
            w = z_ref[b, k] - shift
            w_ref[b, k] = w
            top = jnp.max(fold_rows(w, jnp.maximum), axis=0, keepdims=True)
            total = fold_rows(jnp.exp2(w - top), jnp.add)
            old = peaks[t]
            new = jnp.maximum(old, top)
            peaks[t] = new
            sums[t] = sums[t] * jnp.exp2(old - new) + total * jnp.exp2(top - new)

    for t in range(tgt_blocks):
        total = jnp.sum(sums[t], axis=0, keepdims=True)
        lse = jnp.where(total > 0.0, peaks[t, 0:1, :] + jnp.log2(total), NEGATIVE)
        sums[t] = jnp.broadcast_to(lse, (SUB, BLK))
    spread(cols, sums, cols.shape[0])


def row_totals(table, tile, totals, src_blocks, slots):
    @pl.loop(0, src_blocks, unroll=2)
    def _(b):
        total = None
        for k in range(slots):
            t = table[b * slots + k]
            part = fold_lanes(tile(b, k, t), jnp.add)
            total = part if total is None else total + part
        totals[b] = jnp.broadcast_to(lane_total(total), (SUB, BLK))


def first_row_kernel(table, w_ref, col_parts, q_ref, rows, totals):
    src_blocks = totals.shape[0]
    col_lse = q_ref.at[src_blocks, 1]
    col_lse[: col_parts.shape[1], :] = merge_lse(col_parts[...])

    def tile(b, k, t):
        q = jnp.exp2(w_ref[b, k] - col_lse[pl.ds(t, 1), :])
        q_ref[b, k] = q
        return q

    row_totals(table, tile, totals, src_blocks, w_ref.shape[1])
    spread(rows, totals, rows.shape[0])


def col_kernel(table, q_ref, row_parts, row_scale, cols, sums, *, share):
    src_blocks, slots, tgt_blocks = row_scale.shape[0], q_ref.shape[1], sums.shape[0]
    row_scale[...] = share / add_parts(row_parts[...])
    sums[...] = jnp.zeros(sums.shape, jnp.float32)

    @pl.loop(0, src_blocks, unroll=2)
    def _(b):
        scale = along_rows(row_scale[pl.ds(b, 1), :])
        for k in range(slots):
            t = table[b * slots + k]
            sums[t] += fold_rows(q_ref[b, k] * scale, jnp.add)

    for t in range(tgt_blocks):
        sums[t] = jnp.broadcast_to(jnp.sum(sums[t], axis=0, keepdims=True), (SUB, BLK))
    spread(cols, sums, cols.shape[0])


def inner_col_kernel(table, q_ref, row_parts, cols, sums, row_scale, *, share):
    col_kernel(table, q_ref, row_parts, row_scale, cols, sums, share=share)


def row_kernel(table, q_ref, col_parts, rows, totals, col_scale):
    col_scale[...] = 1.0 / add_parts(col_parts[...])

    def tile(b, k, t):
        return q_ref[b, k] * col_scale[pl.ds(t, 1), :]

    row_totals(table, tile, totals, totals.shape[0], q_ref.shape[1])
    spread(rows, totals, rows.shape[0])


def block_at(flip, sibling):
    chip, core = lax.div(lax.axis_index("tgt"), 2), lax.rem(lax.axis_index("tgt"), 2)
    return 2 * lax.bitwise_xor(chip, flip) + (1 - core if sibling else core)


def weighted(table, q_ref, col_scale, b):
    slots = q_ref.shape[1]
    entries = [table[b * slots + k] for k in range(slots)]
    return [(t, q_ref[b, k] * col_scale[pl.ds(t, 1), :]) for k, t in enumerate(entries)]


def project(table, q_ref, col_scale, tgt, block, outs, width):
    weights = weighted(table, q_ref, col_scale, block)
    rows = [(t, w.astype(jnp.bfloat16)) for t, w in weights]
    total = functools.reduce(jnp.add, [fold_lanes(w, jnp.add) for _, w in weights])
    mass = jnp.broadcast_to(lane_total(total), (SUB, BLK))
    terms = [jnp.dot(w, tgt[t], preferred_element_type=jnp.float32) for t, w in rows]
    result = functools.reduce(jnp.add, terms)
    for n, out in enumerate(outs):
        out[:BLK, :] = result[:, n * width : (n + 1) * width]
        out[BLK:, :BLK] = mass
        out[BLK:, BLK:] = jnp.zeros((SUB, width - BLK), jnp.float32)


def far_kernel(table, q_ref, col_parts, tgt, col_scale, own, other):
    col_scale[...] = 1.0 / add_parts(col_parts[...])
    block_kernel(2, table, q_ref, col_scale, tgt, own, other)


def block_kernel(flip, table, q_ref, col_scale, tgt, own, other):
    for sibling, out in ((True, other), (False, own)):
        halves = [out.at[0], out.at[1]]
        project(table, q_ref, col_scale, tgt, block_at(flip, sibling), halves, out.shape[2])


def end_kernel(table, q_ref, col_scale, tgt, own, other, row_lse, col_lse):
    block_kernel(0, table, q_ref, col_scale, tgt, own, other)
    aux = q_ref.at[row_lse.shape[0]]
    row_lse[...] = aux[0, : row_lse.shape[0], :]
    col_lse[...] = aux[1, : col_lse.shape[0], :]


def far_sum_kernel(own, other, low, high):
    low[...] = own[0] + other[0]
    high[...] = own[1] + other[1]


def near_sum_kernel(own_first, other_first, own_second, other_second, low, high):
    low[...] = own_first[0] + other_first[0]
    high[...] = own_second[1] + other_second[1]


def relay_sum_kernel(way, own, other, received, out):
    out[...] = own[way] + other[way] + received[...]


def near_kernel(low, high, out):
    out[0] = low[...]
    out[1] = high[...]


def finish_kernel(near, own, other, relay_low, relay_high, out_hbm, out, sems):
    mass = near[0, BLK:] + own[0, BLK:] + other[0, BLK:] + relay_low[BLK:]
    scale = to_sublanes(1.0 / mass[0:1, :BLK])
    width = relay_low.shape[1]
    rows = BLK // sems.shape[0]
    copies = []
    for n in range(sems.shape[0]):
        part = pl.ds(n * rows, rows)
        for way, relay in enumerate((relay_low, relay_high)):
            total = near[way, part] + own[way, part] + other[way, part] + relay[part]
            out[part, way * width : (way + 1) * width] = total * scale[n * rows : (n + 1) * rows]
        copies.append(pltpu.make_async_copy(out.at[part], out_hbm.at[part], sems.at[n]))
        copies[-1].start()
    for copy in copies:
        copy.wait()


def in_vmem(x):
    return pltpu.with_memory_space_constraint(x, pltpu.VMEM)


def in_hbm(x):
    return pltpu.with_memory_space_constraint(x, pltpu.HBM)


def f32(*shape):
    return jax.ShapeDtypeStruct(shape, jnp.float32)


def v32(*shape):
    return pltpu.VMEM(shape, jnp.float32)


def exchange(copies, axis):
    return in_vmem(lax.all_to_all(copies, axis, 0, 0))


def merge_kernel(merge, own, other, tiles, out, kept):
    merged = merge(jnp.concatenate([own[...], other[...]], axis=0))
    for d in range(out.shape[0]):
        out[d] = merged


def exchange_cols(cols, merge, tiles):
    pairs = [(i, i ^ 3) for i in range(X_HALVES**2)]
    sends, tiles = pl.pallas_call(
        functools.partial(merge_kernel, merge),
        in_specs=[VMEM] * 3,
        out_specs=[VMEM] * 2,
        out_shape=[
            v32(lax.axis_size(GATHER), *cols.shape[1:]),
            pltpu.VMEM(tiles.shape, jnp.float32),
        ],
        input_output_aliases={2: 1},
        compiler_params=PARAMS,
        name="merge",
    )(in_vmem(cols), in_vmem(lax.ppermute(in_vmem(cols), X_AXES, pairs)), tiles)
    return exchange(sends, GATHER), in_vmem(tiles)


def local(sources, targets, block_lists, live_counts):
    src_rows, features = sources.shape
    src_blocks = src_rows // BLK
    tgt_blocks = targets.shape[0] // BLK
    slots = block_lists.shape[2]
    n_src, n_gather, n_tgt = (lax.axis_size(a) for a in (SRC, GATHER, "tgt"))
    total_src = src_rows * n_src
    total_tgt = targets.shape[0] * n_tgt
    src_blocked = sources.reshape(src_blocks, BLK, features)
    tgt_blocked = targets.reshape(tgt_blocks, BLK, features)
    lists = (block_lists[:, 0, :].T, live_counts.T)
    tiles = v32(src_blocks + 1, slots, BLK, BLK)
    row_shape, col_shape = v32(src_blocks, BLK), v32(tgt_blocks, BLK)
    row_sends, col_sends = v32(n_tgt, src_blocks, BLK), v32(1, tgt_blocks, BLK)
    row_scratch, col_scratch = v32(src_blocks, SUB, BLK), v32(tgt_blocks, SUB, BLK)

    tgt_vmem, z, rows, table = pl.pallas_call(
        functools.partial(cost_kernel, features=features),
        in_specs=[HBM] * 4,
        out_specs=[VMEM, VMEM, VMEM, SMEM],
        out_shape=[
            pltpu.VMEM(tgt_blocked.shape, jnp.bfloat16),
            tiles,
            row_sends,
            pltpu.SMEM((src_blocks * slots,), jnp.int32),
        ],
        scratch_shapes=[
            pltpu.SMEM((slots, src_blocks), jnp.int32),
            pltpu.SMEM((1, src_blocks), jnp.int32),
            pltpu.SMEM((src_blocks * slots,), jnp.int32),
            pltpu.SMEM((tgt_blocks,), jnp.int32),
            pltpu.VMEM(src_blocked.shape, jnp.bfloat16),
            col_scratch,
            row_scratch,
            pltpu.SemaphoreType.DMA((tgt_blocks + src_blocks,)),
            pltpu.SemaphoreType.DMA((2,)),
        ],
        compiler_params=PARAMS,
        name="cost",
    )(*[in_hbm(x) for x in (*lists, src_blocked, tgt_blocked)])
    table = pltpu.with_memory_space_constraint(table, pltpu.SMEM)

    w, cols = pl.pallas_call(
        first_col_kernel,
        in_specs=[SMEM, VMEM, VMEM],
        out_specs=[VMEM, VMEM],
        out_shape=[tiles, col_sends],
        scratch_shapes=[col_scratch, col_scratch],
        input_output_aliases={1: 0},
        compiler_params=PARAMS,
        name="first_col",
    )(table, in_vmem(z), exchange(rows, "tgt"))

    col_parts, w = exchange_cols(cols, merge_lse, in_vmem(w))
    q, rows = pl.pallas_call(
        first_row_kernel,
        in_specs=[SMEM, VMEM, VMEM],
        out_specs=[VMEM, VMEM],
        out_shape=[tiles, row_sends],
        scratch_shapes=[row_scratch],
        input_output_aliases={1: 0},
        compiler_params=PARAMS,
        name="first_row",
    )(table, w, col_parts)
    q = in_vmem(q)

    for sweep in range(1, ITERS):
        last = sweep == ITERS - 1
        *scales, cols = pl.pallas_call(
            functools.partial(
                col_kernel if last else inner_col_kernel, share=total_tgt / total_src
            ),
            in_specs=[SMEM, VMEM, VMEM],
            out_specs=[VMEM] * (1 + last),
            out_shape=[row_shape] * last + [col_sends],
            scratch_shapes=[col_scratch] + [row_shape] * (not last),
            compiler_params=PARAMS,
            name="col_sums",
        )(table, q, exchange(rows, "tgt"))
        col_parts, q = exchange_cols(cols, add_parts, q)
        if not last:
            rows = pl.pallas_call(
                row_kernel,
                in_specs=[SMEM, VMEM, VMEM],
                out_specs=VMEM,
                out_shape=row_sends,
                scratch_shapes=[row_scratch, col_shape],
                compiler_params=PARAMS,
                name="row_sums",
            )(table, q, col_parts)
    (row_scale,) = scales

    tgt_vmem = in_vmem(tgt_vmem)
    halves = v32(2, BLK + SUB, features // 2)
    half = v32(BLK + SUB, features // 2)

    def send(x, flip):
        return lax.ppermute(x, "tgt", [(t, t ^ flip) for t in range(n_tgt)])

    def swap(x, flip=1):
        return in_vmem(send(x, flip))

    def call(kernel, name, operands, out_shape, spec=VMEM, cost=None):
        return pl.pallas_call(
            kernel,
            in_specs=[spec] + [VMEM] * (len(operands) - 1),
            out_specs=[VMEM] * len(out_shape),
            out_shape=out_shape,
            compiler_params=PARAMS,
            cost_estimate=cost,
            name=name,
        )(*operands)

    col_scale, own_far, other_far = call(
        far_kernel, "far", [table, q, col_parts, tgt_vmem], [col_shape, halves, halves], SMEM
    )
    sides = []
    for flip in (1, 3):
        sides.append(
            call(
                functools.partial(block_kernel, flip),
                "side",
                [table, q, in_vmem(col_scale), tgt_vmem],
                [halves, halves],
                SMEM,
            )
        )
    low, high = call(
        far_sum_kernel, "far_sum", [in_vmem(own_far), swap(other_far)], [half, half]
    )
    (low, high), sides, col_scale = lax.optimization_barrier(((low, high), sides, col_scale))
    low, high = swap(low, 2), swap(high, 6)
    own_end, other_end, row_lse, col_lse = call(
        end_kernel,
        "end",
        [table, q, in_vmem(col_scale), tgt_vmem],
        [halves, halves, f32(src_blocks, BLK), f32(tgt_blocks, BLK)],
        SMEM,
    )
    sides = [(own, swap(other)) for own, other in sides]
    (own_first, other_first), (own_second, other_second) = sides
    near_low, near_high = call(
        near_sum_kernel,
        "near_sum",
        [in_vmem(own_first), other_first, in_vmem(own_second), other_second],
        [half, half],
    )
    near = call(
        near_kernel,
        "near",
        [swap(near_low, 2), swap(near_high, 6)],
        [halves],
        cost=pl.CostEstimate(flops=3 * 10**9, bytes_accessed=0, transcendentals=0),
    )[0]

    def relay(way, own, other, received, flip):
        kernel = functools.partial(relay_sum_kernel, way)
        total = call(kernel, "relay_sum", [in_vmem(own), other, received], [half])[0]
        return swap(total, flip)

    relay_high = relay(1, own_first, other_first, high, 2)
    relay_low = relay(0, own_second, other_second, low, 6)
    mapped = pl.pallas_call(
        finish_kernel,
        in_specs=[VMEM] * 5,
        out_specs=HBM,
        out_shape=f32(BLK, features),
        scratch_shapes=[v32(BLK, features), pltpu.SemaphoreType.DMA((4,))],
        compiler_params=PARAMS,
        name="finish",
    )(in_vmem(near), in_vmem(own_end), swap(other_end), relay_low, relay_high)

    late = (sources, row_lse, col_lse, near)
    late_sources, row_lse, col_lse, _ = lax.optimization_barrier(late)
    src_square = jnp.sum(jnp.square(late_sources.astype(jnp.float32)), -1)
    row_potential = (
        EPSILON * (jnp.log(row_scale) - LN2 * row_lse - math.log(total_src))
    ).reshape(src_rows) + src_square / features
    col_potential = EPSILON * (
        jnp.log(col_scale) - LN2 * col_lse + (math.log(total_src) - math.log(total_tgt))
    )
    return (mapped, row_potential, col_potential.reshape(tgt_blocks * BLK))


def solution(mesh):
    n_src, n_tgt = mesh.shape["src"], mesh.shape["tgt"]
    n_z = n_src // X_HALVES**2
    grid = Mesh(mesh.devices.reshape(n_z, X_HALVES, X_HALVES, n_tgt), (*SRC, "tgt"))
    in_specs = (P(SRC, None), P("tgt", None), P(SRC, "tgt", None), P(SRC, "tgt"))
    out_specs = (P((*SRC, "tgt"), None), P(SRC), P("tgt"))
    return jax.shard_map(local, mesh=grid, in_specs=in_specs, out_specs=out_specs, check_vma=False)
```
